256 devices in a mesh: cuts: 2 (over core), state: 128 (over z, y, x).
Axes of the slice: x: 4, y: 4, z: 8, core: 2. Of those that a mesh axis runs over, the one named last changes fastest.
Arguments:
- initial_states: bfloat16 [512, 32, 48, 128], P(('cuts', 'state')), parts along dimension 0, may hold values from -36 to 36
- potential: float32 [32, 48, 128], replicated, may hold values from -1 to 0
- bounds: int32 [4], P('cuts'), parts along dimension 0, may hold values from -32 to 159, as said below
Outputs:
- orthonormal: float32 [512, 196608], P('cuts', 'state'), parts along dimension 0
The draws below stay inside these ranges and needn't reach their ends.
There are 2 independent parts, one for each index of `cuts`. The reference program is written for one: setup_inputs(seed, part) draws one part's arguments, and reference() takes and returns one part's arrays. A program takes and returns all parts, laid end to end along the dimension named above; an argument that names none is the same for every part. Nothing has to cross between parts.
Inputs may be any that keep to these rules, and one draw needn't show every extreme that they name: `bounds`: the first entry lies in -32 to -17, inside the spectrum of H, and the second in 136 to 159, above it; the anchor -1.125 lies below the spectrum.
All inputs are finite; a program needn't handle non-finite values.
Results may differ from the reference program's by a relative error of at most 0.0003.
Values sent between devices are 32-bit elements; how exact they have to be, the bound alone decides.
A program may use at most 128 MiB of HBM per device.

```python
import math
import jax
import jax.numpy as jnp
from jax import lax

NST = 256
GZ = 32
GX = 48
GY = 128
DEGREE = 16


def draw_initial_states(key, part):
    key_rows, key_cols, key_base = jax.random.split(jax.random.fold_in(key, 11), 3)
    points = GZ * GX * GY
    log_span = math.log(10.0)
    row_scale = 0.3 * jnp.exp(jax.random.uniform(key_rows, (points,), jnp.float32, 0.0, log_span))
    col_scale = 0.3 * jnp.exp(jax.random.uniform(key_cols, (NST,), jnp.float32, 0.0, log_span))
    base_draw = jnp.clip(jax.random.normal(key_base, (NST, points), jnp.float32), -4.0, 4.0)
    values = base_draw * row_scale[None, :] * col_scale[:, None]
    return values.reshape(NST, GZ, GX, GY).astype(jnp.bfloat16)


def draw_bounds(key, part):
    key_low, key_high = jax.random.split(jax.random.fold_in(key, 23))
    low_end = jax.random.randint(key_low, (1,), -32, -16)
    high_end = jax.random.randint(key_high, (1,), 136, 160)
    return jnp.concatenate([low_end, high_end]).astype(jnp.int32)


def setup_inputs(seed: int = 0, part: int = 0) -> dict:
    streams_of = jax.random.split(jax.random.key(seed), 4)
    part_splits = jax.random.split(jax.random.fold_in(streams_of[3], part), 4)
    initial_states = draw_initial_states(jax.random.fold_in(jax.random.fold_in(streams_of[3], part), 71), part)
    potential = jnp.clip(jax.random.uniform(streams_of[1], (GZ, GX, GY), jnp.float32, -1.0, 0.0), -1.0, 0.0)
    bounds = draw_bounds(jax.random.fold_in(jax.random.fold_in(streams_of[3], part), 71), part)
    return {"initial_states": initial_states, "potential": potential, "bounds": bounds}


STENCIL_NEAR = 4.0 / 3.0
STENCIL_FAR = -1.0 / 12.0
STENCIL_SELF = -5.0 / 2.0
ANCHOR_VALUE = -1.125

def laplace_periodic(values, axis_dim):
    near_sum = jnp.roll(values, 1, axis_dim) + jnp.roll(values, -1, axis_dim)
    far_sum = jnp.roll(values, 2, axis_dim) + jnp.roll(values, -2, axis_dim)
    return STENCIL_NEAR * near_sum + STENCIL_FAR * far_sum

def laplace_walled(values):
    extent = values.shape[1]
    padded = jnp.pad(values, ((0, 0), (2, 2), (0, 0), (0, 0)))
    near_sum = padded[:, 1:extent + 1] + padded[:, 3:extent + 3]
    far_sum = padded[:, 0:extent] + padded[:, 4:extent + 4]
    return STENCIL_NEAR * near_sum + STENCIL_FAR * far_sum

def apply_hamiltonian(values, potential):
    laplace = 3.0 * STENCIL_SELF * values + laplace_walled(values)
    laplace = laplace + laplace_periodic(values, 2) + laplace_periodic(values, 3)
    return -0.5 * laplace + potential[None] * values

def filter_states(states, potential, bounds):
    low_end = bounds[0].astype(jnp.float32) / 64.0
    high_end = bounds[1].astype(jnp.float32) / 16.0
    half_width = (high_end - low_end) / 2.0
    centre = (high_end + low_end) / 2.0
    sigma_now = half_width / (ANCHOR_VALUE - centre)
    tau_value = 2.0 / sigma_now
    current = (apply_hamiltonian(states, potential) - centre * states) * (sigma_now / half_width)

    def degree_step(degree, carried):
        previous, current, sigma_now = carried
        sigma_next = 1.0 / (tau_value - sigma_now)
        latest = (apply_hamiltonian(current, potential) - centre * current) * (2.0 * sigma_next / half_width)
        latest = latest - sigma_now * sigma_next * previous
        return (current, latest, sigma_next)
    carried = lax.fori_loop(1, DEGREE, degree_step, (states, current, sigma_now))
    return carried[1]

def reference(initial_states, potential, bounds):
    filtered = filter_states(initial_states.astype(jnp.float32), potential, bounds)
    flat = filtered.reshape(NST, GZ * GX * GY)
    gram = lax.dot_general(flat.astype(jnp.float32), flat.astype(jnp.float32), (((1,), (1,)), ((), ())), precision=lax.Precision.HIGHEST, preferred_element_type=jnp.float32)
    factor = jnp.linalg.cholesky(gram)
    solved = lax.linalg.triangular_solve(factor, flat, left_side=True, lower=True)
    return solved * math.sqrt(GZ * GX * GY)
```

```python
import functools
import math

import jax
import jax.numpy as jnp
from jax import lax
from jax.experimental import pallas as pl
from jax.experimental.pallas import tpu as pltpu
from jax.sharding import PartitionSpec as P

DEGREE = 16
ANCHOR_VALUE = -1.125
XB = 8
GY = 128


def chebyshev_scalars(bounds_ref):
    low_end = jnp.full((8, GY), bounds_ref[0].astype(jnp.float32), jnp.float32) / 64.0
    high_end = jnp.full((8, GY), bounds_ref[1].astype(jnp.float32), jnp.float32) / 16.0
    half_width = (high_end - low_end) / 2.0
    centre = (high_end + low_end) / 2.0
    place = (ANCHOR_VALUE - centre) / half_width
    before, now = jnp.ones_like(place), place
    for _ in range(DEGREE - 1):
        before, now = now, 2.0 * place * now - before
    return half_width, centre, 1.0 / now


def circulant():
    row = lax.rem(lax.broadcasted_iota(jnp.int32, (2 * GY, GY), 0), GY)
    column = lax.broadcasted_iota(jnp.int32, (2 * GY, GY), 1)
    apart = lax.rem(row - column + GY, GY)
    near = jnp.where((apart == 1) | (apart == GY - 1), -16.0, 0.0)
    far = jnp.where((apart == 2) | (apart == GY - 2), 1.0, 0.0)
    return (near + far).astype(jnp.bfloat16)


def filter_step(source, target, diagonal, matrix, factor, scale):
    planes, rows = diagonal.shape[0], diagonal.shape[1]
    values = source[pl.ds(2, planes)].reshape(planes * rows * 8, GY)
    high = values.astype(jnp.bfloat16)
    low = (values - high.astype(jnp.float32)).astype(jnp.bfloat16)
    along_y = jnp.dot(
        jnp.concatenate([high, low], 1), matrix, preferred_element_type=jnp.float32
    ).reshape(planes, rows, 8, GY)
    for z in range(planes):
        here = [source[z + 2, r] for r in range(rows)]
        ring = (
            [pltpu.roll(here[r], 1, 0) for r in (rows - 2, rows - 1)]
            + here
            + [pltpu.roll(here[r], 7, 0) for r in (0, 1)]
        )
        for r in range(rows):
            near = (source[z + 1, r] + source[z + 3, r]) + (ring[r + 1] + ring[r + 3])
            far = (source[z, r] + source[z + 4, r]) + (ring[r] + ring[r + 4])
            total = far - 16.0 * near + diagonal[z, r] * here[r] + along_y[z, r]
            latest = factor * total - target[z + 2, r]
            if scale is not None:
                latest = latest * scale
            target[z + 2, r] = latest


def filter_kernel(bounds_ref, states_ref, potential_ref, out_ref, buffers, diagonal, plane):
    states, planes, width, _ = states_ref.shape
    rows = width // 8
    half_width, centre, last_scale = chebyshev_scalars(bounds_ref)
    shift = 3.75 - centre
    factor = 2.0 / (24.0 * half_width)
    zero = jnp.zeros((rows, 8, GY), jnp.float32)

    def load_potential(z, _):
        for r in range(rows):
            diagonal[z, r] = 24.0 * (potential_ref[z, pl.ds(r, 8, stride=rows), :] + shift)
        return 0

    lax.fori_loop(0, planes, load_potential, 0)
    for buffer in range(2):
        for z in (0, 1, planes + 2, planes + 3):
            buffers[buffer, z] = zero
    even, odd = buffers.at[0], buffers.at[1]
    matrix = circulant()

    def one_state(state, _):
        def load(z, _):
            plane[...] = states_ref[state, z].astype(jnp.float32)
            for r in range(rows):
                even[z + 2, r] = plane[pl.ds(r, 8, stride=rows), :]
            odd[z + 2] = zero
            return 0

        lax.fori_loop(0, planes, load, 0)

        def two_steps(pair, _):
            first = jnp.where(pair == 0, 0.5 * factor, factor)
            filter_step(even, odd, diagonal, matrix, first, None)
            last = jnp.where(pair == DEGREE // 2 - 1, last_scale, 1.0)
            filter_step(odd, even, diagonal, matrix, factor, last)
            return 0

        lax.fori_loop(0, DEGREE // 2, two_steps, 0)

        def store(z, _):
            for r in range(rows):
                out_ref[state, z, pl.ds(r, 8, stride=rows), :] = even[z + 2, r]
            return 0

        lax.fori_loop(0, planes, store, 0)
        return 0

    lax.fori_loop(0, states, one_state, 0)


def filter_states(states, potential, bounds):
    planes, width = states.shape[1:3]
    return pl.pallas_call(
        filter_kernel,
        out_shape=jax.ShapeDtypeStruct(states.shape, jnp.float32),
        in_specs=[
            pl.BlockSpec(memory_space=pltpu.SMEM),
            pl.BlockSpec(memory_space=pltpu.VMEM),
            pl.BlockSpec(memory_space=pltpu.VMEM),
        ],
        out_specs=pl.BlockSpec(memory_space=pltpu.VMEM),
        scratch_shapes=[
            pltpu.VMEM((2, planes + 4, width // 8, 8, GY), jnp.float32),
            pltpu.VMEM((planes, width // 8, 8, GY), jnp.float32),
            pltpu.VMEM((width, GY), jnp.float32),
        ],
        compiler_params=pltpu.CompilerParams(vmem_limit_bytes=40 << 20),
        name="chebyshev_filter",
    )(bounds, states, potential)


def per_device(initial_states, potential, bounds):
    filtered = filter_states(initial_states, potential, bounds)
    devices = lax.axis_size("state")
    points = filtered.shape[1] * filtered.shape[2] * filtered.shape[3]
    pieces = filtered.reshape(filtered.shape[0], devices, points // devices // GY, GY)
    gathered = lax.all_to_all(pieces, "state", split_axis=1, concat_axis=0, tiled=True)
    row_block = gathered.reshape(-1, points // devices)
    gram_local = lax.dot_general(
        row_block,
        row_block,
        (((1,), (1,)), ((), ())),
        precision=lax.Precision.HIGHEST,
        preferred_element_type=jnp.float32,
    )
    gram = lax.psum(gram_local, "state")
    factor = jnp.linalg.cholesky(gram)
    solved = lax.linalg.triangular_solve(factor, row_block, left_side=True, lower=True)
    return solved * math.sqrt(points)


def solution(mesh):
    return jax.shard_map(
        per_device,
        mesh=mesh,
        in_specs=(P(("cuts", "state"), None, None, None), P(), P("cuts")),
        out_specs=P("cuts", "state"),
        check_vma=False,
    )
```

```python
import functools
import math

import jax
import jax.numpy as jnp
from jax import lax
from jax.experimental import pallas as pl
from jax.experimental.pallas import tpu as pltpu
from jax.sharding import PartitionSpec as P

DEGREE = 16
ANCHOR_VALUE = -1.125
XB = 8
GY = 128


def chebyshev_scalars(bounds_ref):
    low_end = jnp.full((8, GY), bounds_ref[0].astype(jnp.float32), jnp.float32) / 64.0
    high_end = jnp.full((8, GY), bounds_ref[1].astype(jnp.float32), jnp.float32) / 16.0
    half_width = (high_end - low_end) / 2.0
    centre = (high_end + low_end) / 2.0
    place = (ANCHOR_VALUE - centre) / half_width
    before, now = jnp.ones_like(place), place
    for _ in range(DEGREE - 1):
        before, now = now, 2.0 * place * now - before
    return half_width, centre, 1.0 / now


def circulant():
    row = lax.rem(lax.broadcasted_iota(jnp.int32, (2 * GY, GY), 0), GY)
    column = lax.broadcasted_iota(jnp.int32, (2 * GY, GY), 1)
    apart = lax.rem(row - column + GY, GY)
    near = jnp.where((apart == 1) | (apart == GY - 1), -16.0, 0.0)
    far = jnp.where((apart == 2) | (apart == GY - 2), 1.0, 0.0)
    return (near + far).astype(jnp.bfloat16)


def filter_step(source, target, diagonal, matrix, factor, scale):
    planes, rows = diagonal.shape[0], diagonal.shape[1]
    values = source[pl.ds(2, planes)].reshape(planes * rows * 8, GY)
    high = values.astype(jnp.bfloat16)
    low = (values - high.astype(jnp.float32)).astype(jnp.bfloat16)
    along_y = jnp.dot(
        jnp.concatenate([high, low], 1), matrix, preferred_element_type=jnp.float32
    ).reshape(planes, rows, 8, GY)
    for z in range(planes):
        here = [source[z + 2, r] for r in range(rows)]
        ring = (
            [pltpu.roll(here[r], 1, 0) for r in (rows - 2, rows - 1)]
            + here
            + [pltpu.roll(here[r], 7, 0) for r in (0, 1)]
        )
        for r in range(rows):
            near = (source[z + 1, r] + source[z + 3, r]) + (ring[r + 1] + ring[r + 3])
            far = (source[z, r] + source[z + 4, r]) + (ring[r] + ring[r + 4])
            total = far - 16.0 * near + diagonal[z, r] * here[r] + along_y[z, r]
            latest = factor * total - target[z + 2, r]
            if scale is not None:
                latest = latest * scale
            target[z + 2, r] = latest


PLANES_Z = 8
PLANE_XY = 16


def neighbour(me, number):
    dz, dy, dx = lax.rem(number, 8), lax.rem(lax.div(number, 8), 4), lax.div(number, 32)
    z, y, x = lax.div(me, 16), lax.rem(lax.div(me, 4), 4), lax.rem(me, 4)
    return lax.rem(z + dz, 8) * 16 + lax.rem(y + dy, 4) * 4 + lax.rem(x + dx, 4)


def remote(source, target, send, receive, peer):
    return pltpu.make_async_remote_copy(
        src_ref=source,
        dst_ref=target,
        send_sem=send,
        recv_sem=receive,
        device_id={"state": peer},
        device_id_type=pl.DeviceIdType.MESH,
    )


def wait_bytes(ref, semaphore):
    pltpu.make_async_copy(ref, ref, semaphore).wait()


def filter_gram_kernel(
    bounds_ref,
    states_ref,
    potential_ref,
    rows_ref,
    gram_ref,
    buffers,
    diagonal,
    plane,
    outbox,
    inbox,
    block,
    partial,
    in_plane,
    in_column,
    gathered,
    send_sem,
    recv_sem,
    own_sem,
    rows_sem,
    sum_send,
    sum_recv,
):
    states, planes, width, _ = states_ref.shape
    rows = width // 8
    devices = 128
    piece = planes * width // devices
    me = lax.axis_index("state")

    barrier = pltpu.get_barrier_semaphore()

    def greet(number, _):
        pl.semaphore_signal(
            barrier,
            inc=1,
            device_id={"state": neighbour(me, number)},
            device_id_type=pl.DeviceIdType.MESH,
        )
        return 0

    lax.fori_loop(1, devices, greet, 0)

    half_width, centre, last_scale = chebyshev_scalars(bounds_ref)
    shift = 3.75 - centre
    factor = 2.0 / (24.0 * half_width)
    zero = jnp.zeros((rows, 8, GY), jnp.float32)

    def load_potential(z, _):
        for r in range(rows):
            diagonal[z, r] = 24.0 * (potential_ref[z, pl.ds(r, 8, stride=rows), :] + shift)
        return 0

    lax.fori_loop(0, planes, load_potential, 0)
    for buffer in range(2):
        for z in (0, 1, planes + 2, planes + 3):
            buffers[buffer, z] = zero
    even, odd = buffers.at[0], buffers.at[1]
    matrix = circulant()

    def one_state(state, _):
        def load(z, _):
            plane[...] = states_ref[state, z].astype(jnp.float32)
            for r in range(rows):
                even[z + 2, r] = plane[pl.ds(r, 8, stride=rows), :]
            odd[z + 2] = zero
            return 0

        lax.fori_loop(0, planes, load, 0)

        def two_steps(pair, _):
            first = jnp.where(pair == 0, 0.5 * factor, factor)
            filter_step(even, odd, diagonal, matrix, first, None)
            last = jnp.where(pair == DEGREE // 2 - 1, last_scale, 1.0)
            filter_step(odd, even, diagonal, matrix, factor, last)
            return 0

        lax.fori_loop(0, DEGREE // 2, two_steps, 0)

        def store(z, _):
            for r in range(rows):
                outbox[pl.ds(state * planes * width + z * width + r, 8, stride=rows), :] = even[z + 2, r]
            return 0

        lax.fori_loop(0, planes, store, 0)

        @pl.when(state == 0)
        def _():
            pl.semaphore_wait(barrier, devices - 1)

        def send(number, _):
            peer = neighbour(me, number)
            remote(
                outbox.at[pl.ds((state * devices + peer) * piece, piece)],
                inbox.at[pl.ds((me * states + state) * piece, piece)],
                send_sem,
                recv_sem,
                peer,
            ).start()
            return 0

        lax.fori_loop(1, devices, send, 0)
        pltpu.make_async_copy(
            outbox.at[pl.ds((state * devices + me) * piece, piece)],
            inbox.at[pl.ds((me * states + state) * piece, piece)],
            own_sem.at[state],
        ).start()
        return 0

    lax.fori_loop(0, states, one_state, 0)
    for state in range(states):
        pltpu.make_async_copy(
            outbox.at[pl.ds((state * devices + me) * piece, piece)],
            inbox.at[pl.ds((me * states + state) * piece, piece)],
            own_sem.at[state],
        ).wait()
    wait_bytes(inbox.at[pl.ds(0, (devices - 1) * states * piece)], recv_sem)
    wait_bytes(outbox.at[pl.ds(0, (devices - 1) * states * piece)], send_sem)

    total = devices * states

    def gram_piece(column, _):
        here = inbox[pl.ds(column, total, stride=piece), :]
        block[:, pl.ds(pl.multiple_of(column * GY, GY), GY)] = here
        return 0

    lax.fori_loop(0, piece, gram_piece, 0)
    rows_copy = pltpu.make_async_copy(block, rows_ref, rows_sem)
    rows_copy.start()
    half = total // 2

    def product(left, right):
        return lax.dot_general(
            left,
            right,
            (((1,), (1,)), ((), ())),
            precision=lax.Precision.HIGHEST,
            preferred_element_type=jnp.float32,
        )

    partial[0:half] = product(block[0:half], block[0:half])
    partial[half : 2 * half] = product(block[half:], block[0:half])
    partial[2 * half : 3 * half] = product(block[half:], block[half:])

    count = 3 * half // PLANE_XY
    mine, level = lax.rem(me, PLANE_XY), lax.div(me, PLANE_XY)

    def plane_peer(number):
        y, x = lax.div(mine, 4), lax.rem(mine, 4)
        return lax.rem(y + lax.div(number, 4), 4) * 4 + lax.rem(x + lax.rem(number, 4), 4)

    def share(number, _):
        to = plane_peer(number)
        remote(
            partial.at[pl.ds(pl.multiple_of(to * count, 8), count)],
            in_plane.at[mine],
            sum_send.at[0],
            sum_recv.at[0],
            level * PLANE_XY + to,
        ).start()
        return 0

    lax.fori_loop(1, PLANE_XY, share, 0)
    in_plane[mine] = partial[pl.ds(pl.multiple_of(mine * count, 8), count), :]
    wait_bytes(in_plane.at[pl.ds(0, PLANE_XY - 1)], sum_recv.at[0])
    summed = in_plane[0]
    for number in range(1, PLANE_XY):
        summed = summed + in_plane[number]
    in_column[level] = summed

    def along_z(number, _):
        to = lax.rem(level + number, PLANES_Z)
        remote(
            in_column.at[level],
            in_column.at[level],
            sum_send.at[1],
            sum_recv.at[1],
            to * PLANE_XY + mine,
        ).start()
        return 0

    lax.fori_loop(1, PLANES_Z, along_z, 0)
    wait_bytes(in_column.at[pl.ds(0, PLANES_Z - 1)], sum_recv.at[1])
    summed = in_column[0]
    for number in range(1, PLANES_Z):
        summed = summed + in_column[number]
    here = pl.ds(pl.multiple_of(mine * count, 8), count)
    gathered[here, :] = summed

    def spread(number, _):
        remote(
            gathered.at[here],
            gathered.at[here],
            sum_send.at[2],
            sum_recv.at[2],
            level * PLANE_XY + plane_peer(number),
        ).start()
        return 0

    lax.fori_loop(1, PLANE_XY, spread, 0)
    wait_bytes(gathered.at[pl.ds(0, count * (PLANE_XY - 1))], sum_recv.at[2])
    gram_ref[0:half, 0:half] = gathered[0:half]
    gram_ref[half:, 0:half] = gathered[half : 2 * half]
    gram_ref[0:half, half:] = gathered[half : 2 * half].T
    gram_ref[half:, half:] = gathered[2 * half :]
    wait_bytes(in_plane.at[pl.ds(0, PLANE_XY - 1)], sum_send.at[0])
    wait_bytes(in_column.at[pl.ds(0, PLANES_Z - 1)], sum_send.at[1])
    wait_bytes(gathered.at[pl.ds(0, count * (PLANE_XY - 1))], sum_send.at[2])
    rows_copy.wait()


def filter_and_gram(states, potential, bounds):
    count, planes, width = states.shape[:3]
    total = count * 128
    points = planes * width * GY // 128
    return pl.pallas_call(
        filter_gram_kernel,
        out_shape=[
            jax.ShapeDtypeStruct((total, points), jnp.float32),
            jax.ShapeDtypeStruct((total, total), jnp.float32),
        ],
        in_specs=[
            pl.BlockSpec(memory_space=pltpu.SMEM),
            pl.BlockSpec(memory_space=pltpu.VMEM),
            pl.BlockSpec(memory_space=pltpu.VMEM),
        ],
        out_specs=[pl.BlockSpec(memory_space=pl.ANY), pl.BlockSpec(memory_space=pltpu.VMEM)],
        scratch_shapes=[
            pltpu.VMEM((2, planes + 4, width // 8, 8, GY), jnp.float32),
            pltpu.VMEM((planes, width // 8, 8, GY), jnp.float32),
            pltpu.VMEM((width, GY), jnp.float32),
            pltpu.VMEM((count * planes * width, GY), jnp.float32),
            pltpu.VMEM((count * planes * width, GY), jnp.float32),
            pltpu.VMEM((total, points), jnp.float32),
            pltpu.VMEM((total * 3 // 2, GY), jnp.float32),
            pltpu.VMEM((PLANE_XY, total * 3 // 2 // PLANE_XY, GY), jnp.float32),
            pltpu.VMEM((PLANES_Z, total * 3 // 2 // PLANE_XY, GY), jnp.float32),
            pltpu.VMEM((total * 3 // 2, GY), jnp.float32),
            pltpu.SemaphoreType.DMA,
            pltpu.SemaphoreType.DMA,
            pltpu.SemaphoreType.DMA((count,)),
            pltpu.SemaphoreType.DMA,
            pltpu.SemaphoreType.DMA((3,)),
            pltpu.SemaphoreType.DMA((3,)),
        ],
        compiler_params=pltpu.CompilerParams(
            vmem_limit_bytes=40 << 20, collective_id=0, has_side_effects=True
        ),
        name="filter_and_gram",
    )(bounds, states, potential)


def per_device(initial_states, potential, bounds):
    row_block, gram = filter_and_gram(initial_states, potential, bounds)
    factor = jnp.linalg.cholesky(gram)
    solved = lax.linalg.triangular_solve(factor, row_block, left_side=True, lower=True)
    return solved * math.sqrt(math.prod(initial_states.shape[1:]))


def solution(mesh):
    return jax.shard_map(
        per_device,
        mesh=mesh,
        in_specs=(P(("cuts", "state"), None, None, None), P(), P("cuts")),
        out_specs=P("cuts", "state"),
        check_vma=False,
    )
```

```python
import functools
import math

import jax
import jax.numpy as jnp
from jax import lax
from jax.experimental import pallas as pl
from jax.experimental.pallas import tpu as pltpu
from jax.sharding import PartitionSpec as P

DEGREE = 16
ANCHOR_VALUE = -1.125
XB = 8
GY = 128


def chebyshev_scalars(bounds_ref):
    low_end = jnp.full((8, GY), bounds_ref[0].astype(jnp.float32), jnp.float32) / 64.0
    high_end = jnp.full((8, GY), bounds_ref[1].astype(jnp.float32), jnp.float32) / 16.0
    half_width = (high_end - low_end) / 2.0
    centre = (high_end + low_end) / 2.0
    place = (ANCHOR_VALUE - centre) / half_width
    before, now = jnp.ones_like(place), place
    for _ in range(DEGREE - 1):
        before, now = now, 2.0 * place * now - before
    return half_width, centre, 1.0 / now


def circulant():
    row = lax.rem(lax.broadcasted_iota(jnp.int32, (2 * GY, GY), 0), GY)
    column = lax.broadcasted_iota(jnp.int32, (2 * GY, GY), 1)
    apart = lax.rem(row - column + GY, GY)
    near = jnp.where((apart == 1) | (apart == GY - 1), -16.0, 0.0)
    far = jnp.where((apart == 2) | (apart == GY - 2), 1.0, 0.0)
    return (near + far).astype(jnp.bfloat16)


def filter_step(source, target, diagonal, matrix, factor, scale):
    planes, rows = diagonal.shape[0], diagonal.shape[1]
    values = source[pl.ds(2, planes)].reshape(planes * rows * 8, GY)
    high = values.astype(jnp.bfloat16)
    low = (values - high.astype(jnp.float32)).astype(jnp.bfloat16)
    along_y = jnp.dot(
        jnp.concatenate([high, low], 1), matrix, preferred_element_type=jnp.float32
    ).reshape(planes, rows, 8, GY)
    for z in range(planes):
        here = [source[z + 2, r] for r in range(rows)]
        ring = (
            [pltpu.roll(here[r], 1, 0) for r in (rows - 2, rows - 1)]
            + here
            + [pltpu.roll(here[r], 7, 0) for r in (0, 1)]
        )
        for r in range(rows):
            near = (source[z + 1, r] + source[z + 3, r]) + (ring[r + 1] + ring[r + 3])
            far = (source[z, r] + source[z + 4, r]) + (ring[r] + ring[r + 4])
            total = far - 16.0 * near + diagonal[z, r] * here[r] + along_y[z, r]
            latest = factor * total - target[z + 2, r]
            if scale is not None:
                latest = latest * scale
            target[z + 2, r] = latest


PLANES_Z = 8
PLANE_XY = 16


def neighbour(me, number):
    dz, dy, dx = lax.rem(number, 8), lax.rem(lax.div(number, 8), 4), lax.div(number, 32)
    z, y, x = lax.div(me, 16), lax.rem(lax.div(me, 4), 4), lax.rem(me, 4)
    return lax.rem(z + dz, 8) * 16 + lax.rem(y + dy, 4) * 4 + lax.rem(x + dx, 4)


def along(me, stride, extent, number):
    place = lax.rem(lax.div(me, stride), extent)
    return me + (lax.rem(place + number, extent) - place) * stride


def greet(semaphore, me, stride, extent):
    for number in range(1, extent):
        pl.semaphore_signal(
            semaphore,
            inc=1,
            device_id={"state": along(me, stride, extent, number)},
            device_id_type=pl.DeviceIdType.MESH,
        )


def remote(source, target, send, receive, peer):
    return pltpu.make_async_remote_copy(
        src_ref=source,
        dst_ref=target,
        send_sem=send,
        recv_sem=receive,
        device_id={"state": peer},
        device_id_type=pl.DeviceIdType.MESH,
    )


def wait_bytes(ref, semaphore):
    pltpu.make_async_copy(ref, ref, semaphore).wait()


def filter_gram_kernel(
    bounds_ref,
    states_ref,
    potential_ref,
    rows_ref,
    gram_ref,
    initial,
    potential,
    buffers,
    diagonal,
    plane,
    outbox,
    inbox,
    block,
    partial,
    in_plane,
    in_column,
    gathered,
    send_sem,
    recv_sem,
    own_sem,
    rows_sem,
    sum_send,
    sum_recv,
    load_sem,
    heard_x,
    heard_y,
):
    states, planes, width, _ = states_ref.shape
    rows = width // 8
    devices = 128
    piece = planes * width // devices
    me = lax.axis_index("state")

    loads = [
        pltpu.make_async_copy(potential_ref, potential, load_sem.at[states]),
    ] + [
        pltpu.make_async_copy(states_ref.at[state], initial.at[state], load_sem.at[state])
        for state in range(states)
    ]
    for load in loads:
        load.start()

    barrier = pltpu.get_barrier_semaphore()
    greet(barrier, me, 16, 8)
    greet(barrier, me, 4, 4)
    greet(barrier, me, 1, 4)

    half_width, centre, last_scale = chebyshev_scalars(bounds_ref)
    shift = 3.75 - centre
    factor = 2.0 / (24.0 * half_width)
    zero = jnp.zeros((rows, 8, GY), jnp.float32)

    def load_potential(z, _):
        for r in range(rows):
            diagonal[z, r] = 24.0 * (potential[z, pl.ds(r, 8, stride=rows), :] + shift)
        return 0

    for buffer in range(2):
        for z in (0, 1, planes + 2, planes + 3):
            buffers[buffer, z] = zero
    loads[0].wait()
    lax.fori_loop(0, planes, load_potential, 0)
    pl.semaphore_wait(barrier, 7 + 3 + 3)
    greet(heard_x, me, 1, 4)
    for load in loads[1:]:
        load.wait()
    even, odd = buffers.at[0], buffers.at[1]
    matrix = circulant()

    def one_state(state, _):
        def load(z, _):
            plane[...] = initial[state, z].astype(jnp.float32)
            for r in range(rows):
                even[z + 2, r] = plane[pl.ds(r, 8, stride=rows), :]
            odd[z + 2] = zero
            return 0

        lax.fori_loop(0, planes, load, 0)

        def two_steps(pair, _):
            first = jnp.where(pair == 0, 0.5 * factor, factor)
            filter_step(even, odd, diagonal, matrix, first, None)

            @pl.when((state == 0) & (pair == 3))
            def _():
                pl.semaphore_wait(heard_x, 3)
                greet(heard_y, me, 4, 4)

            last = jnp.where(pair == DEGREE // 2 - 1, last_scale, 1.0)
            filter_step(odd, even, diagonal, matrix, factor, last)
            return 0

        lax.fori_loop(0, DEGREE // 2, two_steps, 0)

        def store(z, _):
            for r in range(rows):
                outbox[pl.ds(state * planes * width + z * width + r, 8, stride=rows), :] = even[z + 2, r]
            return 0

        lax.fori_loop(0, planes, store, 0)

        @pl.when(state == 0)
        def _():
            pl.semaphore_wait(heard_y, 3)

        def send(number, _):
            peer = neighbour(me, number)
            remote(
                outbox.at[pl.ds((state * devices + peer) * piece, piece)],
                inbox.at[pl.ds((me * states + state) * piece, piece)],
                send_sem,
                recv_sem,
                peer,
            ).start()
            return 0

        lax.fori_loop(1, devices, send, 0)
        pltpu.make_async_copy(
            outbox.at[pl.ds((state * devices + me) * piece, piece)],
            inbox.at[pl.ds((me * states + state) * piece, piece)],
            own_sem.at[state],
        ).start()
        return 0

    lax.fori_loop(0, states, one_state, 0)
    for state in range(states):
        pltpu.make_async_copy(
            outbox.at[pl.ds((state * devices + me) * piece, piece)],
            inbox.at[pl.ds((me * states + state) * piece, piece)],
            own_sem.at[state],
        ).wait()
    wait_bytes(inbox.at[pl.ds(0, (devices - 1) * states * piece)], recv_sem)
    wait_bytes(outbox.at[pl.ds(0, (devices - 1) * states * piece)], send_sem)

    total = devices * states

    def gram_piece(column, _):
        here = inbox[pl.ds(column, total, stride=piece), :]
        block[:, pl.ds(pl.multiple_of(column * GY, GY), GY)] = here
        return 0

    lax.fori_loop(0, piece, gram_piece, 0)
    rows_copy = pltpu.make_async_copy(block, rows_ref, rows_sem)
    rows_copy.start()
    half = total // 2

    def product(left, right):
        return lax.dot_general(
            left,
            right,
            (((1,), (1,)), ((), ())),
            precision=lax.Precision.HIGHEST,
            preferred_element_type=jnp.float32,
        )

    partial[0:half] = product(block[0:half], block[0:half])
    partial[half : 2 * half] = product(block[half:], block[0:half])
    partial[2 * half : 3 * half] = product(block[half:], block[half:])

    count = 3 * half // PLANE_XY
    mine, level = lax.rem(me, PLANE_XY), lax.div(me, PLANE_XY)

    def plane_peer(number):
        y, x = lax.div(mine, 4), lax.rem(mine, 4)
        return lax.rem(y + lax.div(number, 4), 4) * 4 + lax.rem(x + lax.rem(number, 4), 4)

    def share(number, _):
        to = plane_peer(number)
        remote(
            partial.at[pl.ds(pl.multiple_of(to * count, 8), count)],
            in_plane.at[mine],
            sum_send.at[0],
            sum_recv.at[0],
            level * PLANE_XY + to,
        ).start()
        return 0

    lax.fori_loop(1, PLANE_XY, share, 0)
    in_plane[mine] = partial[pl.ds(pl.multiple_of(mine * count, 8), count), :]
    wait_bytes(in_plane.at[pl.ds(0, PLANE_XY - 1)], sum_recv.at[0])
    summed = in_plane[0]
    for number in range(1, PLANE_XY):
        summed = summed + in_plane[number]
    in_column[level] = summed

    def along_z(number, _):
        to = lax.rem(level + number, PLANES_Z)
        remote(
            in_column.at[level],
            in_column.at[level],
            sum_send.at[1],
            sum_recv.at[1],
            to * PLANE_XY + mine,
        ).start()
        return 0

    lax.fori_loop(1, PLANES_Z, along_z, 0)
    wait_bytes(in_column.at[pl.ds(0, PLANES_Z - 1)], sum_recv.at[1])
    summed = in_column[0]
    for number in range(1, PLANES_Z):
        summed = summed + in_column[number]
    here = pl.ds(pl.multiple_of(mine * count, 8), count)
    gathered[here, :] = summed

    def spread(number, _):
        remote(
            gathered.at[here],
            gathered.at[here],
            sum_send.at[2],
            sum_recv.at[2],
            level * PLANE_XY + plane_peer(number),
        ).start()
        return 0

    lax.fori_loop(1, PLANE_XY, spread, 0)
    wait_bytes(gathered.at[pl.ds(0, count * (PLANE_XY - 1))], sum_recv.at[2])
    gram_ref[0:half, 0:half] = gathered[0:half]
    gram_ref[half:, 0:half] = gathered[half : 2 * half]
    gram_ref[0:half, half:] = gathered[half : 2 * half].T
    gram_ref[half:, half:] = gathered[2 * half :]
    wait_bytes(in_plane.at[pl.ds(0, PLANE_XY - 1)], sum_send.at[0])
    wait_bytes(in_column.at[pl.ds(0, PLANES_Z - 1)], sum_send.at[1])
    wait_bytes(gathered.at[pl.ds(0, count * (PLANE_XY - 1))], sum_send.at[2])
    rows_copy.wait()


def filter_and_gram(states, potential, bounds):
    count, planes, width = states.shape[:3]
    total = count * 128
    points = planes * width * GY // 128
    return pl.pallas_call(
        filter_gram_kernel,
        out_shape=[
            jax.ShapeDtypeStruct((total, points), jnp.float32),
            jax.ShapeDtypeStruct((total, total), jnp.float32),
        ],
        in_specs=[
            pl.BlockSpec(memory_space=pltpu.SMEM),
            pl.BlockSpec(memory_space=pl.ANY),
            pl.BlockSpec(memory_space=pl.ANY),
        ],
        out_specs=[pl.BlockSpec(memory_space=pl.ANY), pl.BlockSpec(memory_space=pltpu.VMEM)],
        scratch_shapes=[
            pltpu.VMEM(states.shape, states.dtype),
            pltpu.VMEM(potential.shape, potential.dtype),
            pltpu.VMEM((2, planes + 4, width // 8, 8, GY), jnp.float32),
            pltpu.VMEM((planes, width // 8, 8, GY), jnp.float32),
            pltpu.VMEM((width, GY), jnp.float32),
            pltpu.VMEM((count * planes * width, GY), jnp.float32),
            pltpu.VMEM((count * planes * width, GY), jnp.float32),
            pltpu.VMEM((total, points), jnp.float32),
            pltpu.VMEM((total * 3 // 2, GY), jnp.float32),
            pltpu.VMEM((PLANE_XY, total * 3 // 2 // PLANE_XY, GY), jnp.float32),
            pltpu.VMEM((PLANES_Z, total * 3 // 2 // PLANE_XY, GY), jnp.float32),
            pltpu.VMEM((total * 3 // 2, GY), jnp.float32),
            pltpu.SemaphoreType.DMA,
            pltpu.SemaphoreType.DMA,
            pltpu.SemaphoreType.DMA((count,)),
            pltpu.SemaphoreType.DMA,
            pltpu.SemaphoreType.DMA((3,)),
            pltpu.SemaphoreType.DMA((3,)),
            pltpu.SemaphoreType.DMA((count + 1,)),
            pltpu.SemaphoreType.REGULAR,
            pltpu.SemaphoreType.REGULAR,
        ],
        compiler_params=pltpu.CompilerParams(
            vmem_limit_bytes=56 << 20, collective_id=0, has_side_effects=True
        ),
        name="filter_and_gram",
    )(bounds, states, potential)


def times(left, right, left_dim, right_dim):
    return lax.dot_general(
        left,
        right,
        (((left_dim,), (right_dim,)), ((), ())),
        precision=lax.Precision.HIGHEST,
        preferred_element_type=jnp.float32,
    )


def inverse_factor(tiles):
    row = lax.broadcasted_iota(jnp.int32, (8, 128), 0)
    lane = lax.broadcasted_iota(jnp.int32, (8, 128), 1)

    def of_row(value, index):
        return jnp.broadcast_to(value[index : index + 1, :], (8, 128))

    def of_lane(value, index):
        return jnp.broadcast_to(value[:, index : index + 1], (8, 128))

    tiles = list(tiles)
    result = []
    for tile in range(16):
        start = 8 * tile
        here = tiles[tile]
        solved = jnp.zeros((8, 128), jnp.float32)
        columns = [of_lane(here, start + c) for c in range(8)]
        below = range(tile + 1, 16)
        multipliers = [[of_lane(tiles[i], start + c) for c in range(8)] for i in below]
        for i in range(8):
            pivot = of_row(columns[i], i)
            root = lax.rsqrt(pivot)
            root = root * (1.5 - 0.5 * pivot * root * root)
            inverse = root * root
            here = jnp.where(lane == start + i, jnp.where(row == i, 1.0, 0.0), here)
            pivot_row = of_row(here, i)
            solved = jnp.where(row == i, pivot_row * root, solved)
            others = jnp.where(row == i, 0.0, columns[i])
            scaled = pivot_row * inverse
            here = jnp.where(row == i, scaled, here - others * scaled)
            for c in range(i + 1, 8):
                entry = of_row(columns[c], i) * inverse
                columns[c] = jnp.where(row == i, entry, columns[c] - others * entry)
        result.append(jnp.where(lane <= start + row, solved, 0.0))
        spread = [of_row(here, c) for c in range(8)]
        for multiplier, i in zip(multipliers, below):
            parts = [multiplier[c] * spread[c] for c in range(8)]
            total = ((parts[0] + parts[1]) + (parts[2] + parts[3])) + (
                (parts[4] + parts[5]) + (parts[6] + parts[7])
            )
            tiles[i] = jnp.where((lane >= start) & (lane < start + 8), 0.0, tiles[i]) - total
    return result


def factor_and_solve_kernel(
    gram_ref, rows_ref, out_ref, work, inverses, low, rows, out, rows_sem, out_sem, *, scale
):
    half = gram_ref.shape[0] // 2
    width = rows_ref.shape[1]
    load = pltpu.make_async_copy(rows_ref, rows, rows_sem)
    load.start()
    work[...] = gram_ref[0:half, 0:half]

    def one_half(number, _):
        tiles = inverse_factor([work[8 * i : 8 * i + 8] for i in range(16)])
        for i in range(16):
            inverses[number, 8 * i : 8 * i + 8] = tiles[i]

        @pl.when(number == 0)
        def _():
            low[...] = times(gram_ref[half:, 0:half], inverses[0], 1, 1)
            work[...] = gram_ref[half:, half:] - times(low[...], low[...], 1, 1)

        return 0

    lax.fori_loop(0, 2, one_half, 0)
    first, second = inverses[0] * scale, inverses[1] * scale
    between = -times(times(second, low[...], 1, 0), inverses[0], 1, 0)
    load.wait()
    pieces = out_sem.shape[0]
    stores = []
    for piece in range(pieces):
        here = pl.ds(piece * width // pieces, width // pieces)
        upper, lower = rows[0:half, here], rows[half:, here]
        out[0:half, here] = times(first, upper, 1, 0)
        out[half:, here] = times(between, upper, 1, 0) + times(second, lower, 1, 0)
        store = pltpu.make_async_copy(out.at[:, here], out_ref.at[:, here], out_sem.at[piece])
        store.start()
        stores.append(store)
    for store in stores:
        store.wait()


def factor_and_solve(gram, rows, scale):
    half = gram.shape[0] // 2
    return pl.pallas_call(
        functools.partial(factor_and_solve_kernel, scale=scale),
        out_shape=jax.ShapeDtypeStruct(rows.shape, jnp.float32),
        in_specs=[pl.BlockSpec(memory_space=pltpu.VMEM), pl.BlockSpec(memory_space=pl.ANY)],
        out_specs=pl.BlockSpec(memory_space=pl.ANY),
        scratch_shapes=[
            pltpu.VMEM((half, half), jnp.float32),
            pltpu.VMEM((2, half, half), jnp.float32),
            pltpu.VMEM((half, half), jnp.float32),
            pltpu.VMEM(rows.shape, jnp.float32),
            pltpu.VMEM(rows.shape, jnp.float32),
            pltpu.SemaphoreType.DMA,
            pltpu.SemaphoreType.DMA((4,)),
        ],
        compiler_params=pltpu.CompilerParams(vmem_limit_bytes=56 << 20),
        name="factor_and_solve",
    )(gram, rows)


def per_device(initial_states, potential, bounds):
    row_block, gram = filter_and_gram(initial_states, potential, bounds)
    return factor_and_solve(gram, row_block, math.sqrt(math.prod(initial_states.shape[1:])))


def solution(mesh):
    return jax.shard_map(
        per_device,
        mesh=mesh,
        in_specs=(P(("cuts", "state"), None, None, None), P(), P("cuts")),
        out_specs=P("cuts", "state"),
        check_vma=False,
    )
```

```python
import functools
import math

import jax
import jax.numpy as jnp
from jax import lax
from jax.experimental import pallas as pl
from jax.experimental.pallas import tpu as pltpu
from jax.sharding import PartitionSpec as P

DEGREE = 16
ANCHOR_VALUE = -1.125
XB = 8
GY = 128


def chebyshev_scalars(bounds_ref):
    low_end = jnp.full((8, GY), bounds_ref[0].astype(jnp.float32), jnp.float32) / 64.0
    high_end = jnp.full((8, GY), bounds_ref[1].astype(jnp.float32), jnp.float32) / 16.0
    half_width = (high_end - low_end) / 2.0
    centre = (high_end + low_end) / 2.0
    place = (ANCHOR_VALUE - centre) / half_width
    before, now = jnp.ones_like(place), place
    for _ in range(DEGREE - 1):
        before, now = now, 2.0 * place * now - before
    return half_width, centre, 1.0 / now


def circulant():
    row = lax.rem(lax.broadcasted_iota(jnp.int32, (2 * GY, GY), 0), GY)
    column = lax.broadcasted_iota(jnp.int32, (2 * GY, GY), 1)
    apart = lax.rem(row - column + GY, GY)
    near = jnp.where((apart == 1) | (apart == GY - 1), -16.0, 0.0)
    far = jnp.where((apart == 2) | (apart == GY - 2), 1.0, 0.0)
    return (near + far).astype(jnp.bfloat16)


def filter_step(source, target, diagonal, matrix, factor, scale):
    planes, rows = diagonal.shape[0], diagonal.shape[1]
    values = source[pl.ds(2, planes)].reshape(planes * rows * 8, GY)
    high = values.astype(jnp.bfloat16)
    low = (values - high.astype(jnp.float32)).astype(jnp.bfloat16)
    along_y = jnp.dot(
        jnp.concatenate([high, low], 1), matrix, preferred_element_type=jnp.float32
    ).reshape(planes, rows, 8, GY)
    for z in range(planes):
        here = [source[z + 2, r] for r in range(rows)]
        ring = (
            [pltpu.roll(here[r], 1, 0) for r in (rows - 2, rows - 1)]
            + here
            + [pltpu.roll(here[r], 7, 0) for r in (0, 1)]
        )
        for r in range(rows):
            near = (source[z + 1, r] + source[z + 3, r]) + (ring[r + 1] + ring[r + 3])
            far = (source[z, r] + source[z + 4, r]) + (ring[r] + ring[r + 4])
            total = far - 16.0 * near + diagonal[z, r] * here[r] + along_y[z, r]
            latest = factor * total - target[z + 2, r]
            if scale is not None:
                latest = latest * scale
            target[z + 2, r] = latest


GROUP = 4
PLANES_Z = 8
PLANE_XY = 16


def neighbour(me, number):
    dz, dy, dx = lax.rem(number, 8), lax.rem(lax.div(number, 8), 4), lax.div(number, 32)
    z, y, x = lax.div(me, 16), lax.rem(lax.div(me, 4), 4), lax.rem(me, 4)
    return lax.rem(z + dz, 8) * 16 + lax.rem(y + dy, 4) * 4 + lax.rem(x + dx, 4)


def along(me, stride, extent, number):
    place = lax.rem(lax.div(me, stride), extent)
    return me + (lax.rem(place + number, extent) - place) * stride


def greet(semaphore, me, stride, extent):
    for number in range(1, extent):
        pl.semaphore_signal(
            semaphore,
            inc=1,
            device_id={"state": along(me, stride, extent, number)},
            device_id_type=pl.DeviceIdType.MESH,
        )


def remote(source, target, send, receive, peer):
    return pltpu.make_async_remote_copy(
        src_ref=source,
        dst_ref=target,
        send_sem=send,
        recv_sem=receive,
        device_id={"state": peer},
        device_id_type=pl.DeviceIdType.MESH,
    )


def wait_bytes(ref, semaphore):
    pltpu.make_async_copy(ref, ref, semaphore).wait()


def filter_gram_kernel(
    bounds_ref,
    states_ref,
    potential_ref,
    rows_ref,
    first_ref,
    low_ref,
    rest_ref,
    initial,
    potential,
    buffers,
    diagonal,
    plane,
    outbox,
    inbox,
    block,
    partial_first,
    partial_rest,
    plane_first,
    plane_rest,
    column_first,
    column_rest,
    gathered_first,
    gathered_rest,
    send_sem,
    recv_sem,
    own_sem,
    rows_sem,
    sum_send,
    sum_recv,
    load_sem,
    heard_x,
    heard_y,
):
    partial, in_plane = (partial_first, partial_rest), (plane_first, plane_rest)
    in_column, gathered = (column_first, column_rest), (gathered_first, gathered_rest)
    states, planes, width, _ = states_ref.shape
    rows = width // 8
    devices = 128
    piece = planes * width // devices
    me = lax.axis_index("state")

    loads = [
        pltpu.make_async_copy(potential_ref, potential, load_sem.at[states]),
    ] + [
        pltpu.make_async_copy(states_ref.at[state], initial.at[state], load_sem.at[state])
        for state in range(states)
    ]
    for load in loads:
        load.start()

    barrier = pltpu.get_barrier_semaphore()
    greet(barrier, me, 16, 8)
    greet(barrier, me, 4, 4)
    greet(barrier, me, 1, 4)

    half_width, centre, last_scale = chebyshev_scalars(bounds_ref)
    shift = 3.75 - centre
    factor = 2.0 / (24.0 * half_width)
    zero = jnp.zeros((rows, 8, GY), jnp.float32)

    def load_potential(group, _):
        for part in range(GROUP):
            z = group * GROUP + part
            for r in range(rows):
                diagonal[z, r] = 24.0 * (potential[z, pl.ds(r, 8, stride=rows), :] + shift)
        return 0

    for buffer in range(2):
        for z in (0, 1, planes + 2, planes + 3):
            buffers[buffer, z] = zero
    loads[0].wait()
    lax.fori_loop(0, planes // GROUP, load_potential, 0)
    pl.semaphore_wait(barrier, 7 + 3 + 3)
    greet(heard_x, me, 1, 4)
    loads[1].wait()
    even, odd = buffers.at[0], buffers.at[1]
    matrix = circulant()

    def one_state(state, _):
        def load(group, _):
            for part in range(GROUP):
                plane[part] = initial[state, group * GROUP + part].astype(jnp.float32)
            for part in range(GROUP):
                z = group * GROUP + part
                for r in range(rows):
                    even[z + 2, r] = plane[part, pl.ds(r, 8, stride=rows), :]
                odd[z + 2] = zero
            return 0

        lax.fori_loop(0, planes // GROUP, load, 0)

        def two_steps(pair, _):
            first = jnp.where(pair == 0, 0.5 * factor, factor)
            filter_step(even, odd, diagonal, matrix, first, None)

            @pl.when((state == 0) & (pair == 3))
            def _():
                pl.semaphore_wait(heard_x, 3)
                greet(heard_y, me, 4, 4)
                for load in loads[2:]:
                    load.wait()

            last = jnp.where(pair == DEGREE // 2 - 1, last_scale, 1.0)
            filter_step(odd, even, diagonal, matrix, factor, last)
            return 0

        lax.fori_loop(0, DEGREE // 2, two_steps, 0)

        def store(group, _):
            for part in range(GROUP):
                z = group * GROUP + part
                for r in range(rows):
                    outbox[pl.ds((state * planes + z) * width + r, 8, stride=rows), :] = even[z + 2, r]
            return 0

        lax.fori_loop(0, planes // GROUP, store, 0)

        @pl.when(state == 0)
        def _():
            pl.semaphore_wait(heard_y, 3)

        def send(number, _):
            peer = neighbour(me, number)
            remote(
                outbox.at[pl.ds((state * devices + peer) * piece, piece)],
                inbox.at[pl.ds((me * states + state) * piece, piece)],
                send_sem,
                recv_sem,
                peer,
            ).start()
            return 0

        lax.fori_loop(1, devices, send, 0)
        pltpu.make_async_copy(
            outbox.at[pl.ds((state * devices + me) * piece, piece)],
            inbox.at[pl.ds((me * states + state) * piece, piece)],
            own_sem.at[state],
        ).start()
        return 0

    lax.fori_loop(0, states, one_state, 0)
    for state in range(states):
        pltpu.make_async_copy(
            outbox.at[pl.ds((state * devices + me) * piece, piece)],
            inbox.at[pl.ds((me * states + state) * piece, piece)],
            own_sem.at[state],
        ).wait()
    wait_bytes(inbox.at[pl.ds(0, (devices - 1) * states * piece)], recv_sem)
    wait_bytes(outbox.at[pl.ds(0, (devices - 1) * states * piece)], send_sem)

    total = devices * states

    def gram_piece(column, _):
        here = inbox[pl.ds(column, total, stride=piece), :]
        block[:, pl.ds(pl.multiple_of(column * GY, GY), GY)] = here
        return 0

    lax.fori_loop(0, piece, gram_piece, 0)
    rows_copy = pltpu.make_async_copy(block, rows_ref, rows_sem)
    rows_copy.start()
    half = total // 2

    mine, level = lax.rem(me, PLANE_XY), lax.div(me, PLANE_XY)

    def part_of(ref, number):
        count = ref.shape[0] // PLANE_XY
        return pl.ds(pl.multiple_of(number * count, 8), count)

    def plane_peer(number):
        y, x = lax.div(mine, 4), lax.rem(mine, 4)
        return lax.rem(y + lax.div(number, 4), 4) * 4 + lax.rem(x + lax.rem(number, 4), 4)

    def first_round(which):
        source, target = partial[which], in_plane[which]

        def share(number, _):
            to = plane_peer(number)
            remote(
                source.at[part_of(source, to)],
                target.at[mine],
                sum_send.at[which, 0],
                sum_recv.at[which, 0],
                level * PLANE_XY + to,
            ).start()
            return 0

        lax.fori_loop(1, PLANE_XY, share, 0)
        target[mine] = source[part_of(source, mine), :]

    def total_of(ref):
        parts = [ref[number] for number in range(ref.shape[0])]
        while len(parts) > 1:
            parts = [parts[i] + parts[i + 1] for i in range(0, len(parts), 2)]
        return parts[0]

    def second_round(which):
        source, target = in_plane[which], in_column[which]
        wait_bytes(source.at[pl.ds(0, PLANE_XY - 1)], sum_recv.at[which, 0])
        target[level] = total_of(source)

        def along_z(number, _):
            remote(
                target.at[level],
                target.at[level],
                sum_send.at[which, 1],
                sum_recv.at[which, 1],
                lax.rem(level + number, PLANES_Z) * PLANE_XY + mine,
            ).start()
            return 0

        lax.fori_loop(1, PLANES_Z, along_z, 0)

    def third_round(which):
        source, target = in_column[which], gathered[which]
        wait_bytes(source.at[pl.ds(0, PLANES_Z - 1)], sum_recv.at[which, 1])
        here = part_of(target, mine)
        target[here, :] = total_of(source)

        def spread(number, _):
            remote(
                target.at[here],
                target.at[here],
                sum_send.at[which, 2],
                sum_recv.at[which, 2],
                level * PLANE_XY + plane_peer(number),
            ).start()
            return 0

        lax.fori_loop(1, PLANE_XY, spread, 0)

    def most_of(ref):
        return ref.at[pl.ds(0, ref.shape[0] // PLANE_XY * (PLANE_XY - 1))]

    partial[0][...] = times(block[0:half], block[0:half], 1, 1)
    first_round(0)
    partial[1][0:half] = times(block[half:], block[0:half], 1, 1)
    partial[1][half:] = times(block[half:], block[half:], 1, 1)
    first_round(1)
    second_round(0)
    second_round(1)
    third_round(0)
    third_round(1)
    wait_bytes(most_of(gathered[0]), sum_recv.at[0, 2])
    tiles = inverse_factor([gathered[0][8 * i : 8 * i + 8] for i in range(16)])
    for i in range(16):
        first_ref[8 * i : 8 * i + 8] = tiles[i]
    wait_bytes(most_of(gathered[1]), sum_recv.at[1, 2])
    low = times(gathered[1][0:half], first_ref[...], 1, 1)
    low_ref[...] = low
    rest_ref[...] = gathered[1][half:] - times(low, low, 1, 1)
    for which in range(2):
        wait_bytes(in_plane[which].at[pl.ds(0, PLANE_XY - 1)], sum_send.at[which, 0])
        wait_bytes(in_column[which].at[pl.ds(0, PLANES_Z - 1)], sum_send.at[which, 1])
        wait_bytes(most_of(gathered[which]), sum_send.at[which, 2])
    rows_copy.wait()


def filter_and_gram(states, potential, bounds):
    count, planes, width = states.shape[:3]
    total, half = count * 128, count * 64
    points = planes * width * GY // 128
    return pl.pallas_call(
        filter_gram_kernel,
        out_shape=[
            jax.ShapeDtypeStruct((total, points), jnp.float32),
            jax.ShapeDtypeStruct((half, half), jnp.float32),
            jax.ShapeDtypeStruct((half, half), jnp.float32),
            jax.ShapeDtypeStruct((half, half), jnp.float32),
        ],
        in_specs=[
            pl.BlockSpec(memory_space=pltpu.SMEM),
            pl.BlockSpec(memory_space=pl.ANY),
            pl.BlockSpec(memory_space=pl.ANY),
        ],
        out_specs=[pl.BlockSpec(memory_space=pl.ANY)] + [pl.BlockSpec(memory_space=pltpu.VMEM)] * 3,
        scratch_shapes=[
            pltpu.VMEM(states.shape, states.dtype),
            pltpu.VMEM(potential.shape, potential.dtype),
            pltpu.VMEM((2, planes + 4, width // 8, 8, GY), jnp.float32),
            pltpu.VMEM((planes, width // 8, 8, GY), jnp.float32),
            pltpu.VMEM((GROUP, width, GY), jnp.float32),
            pltpu.VMEM((count * planes * width, GY), jnp.float32),
            pltpu.VMEM((count * planes * width, GY), jnp.float32),
            pltpu.VMEM((total, points), jnp.float32),
            pltpu.VMEM((half, GY), jnp.float32),
            pltpu.VMEM((total, GY), jnp.float32),
            pltpu.VMEM((PLANE_XY, half // PLANE_XY, GY), jnp.float32),
            pltpu.VMEM((PLANE_XY, total // PLANE_XY, GY), jnp.float32),
            pltpu.VMEM((PLANES_Z, half // PLANE_XY, GY), jnp.float32),
            pltpu.VMEM((PLANES_Z, total // PLANE_XY, GY), jnp.float32),
            pltpu.VMEM((half, GY), jnp.float32),
            pltpu.VMEM((total, GY), jnp.float32),
            pltpu.SemaphoreType.DMA,
            pltpu.SemaphoreType.DMA,
            pltpu.SemaphoreType.DMA((count,)),
            pltpu.SemaphoreType.DMA,
            pltpu.SemaphoreType.DMA((2, 3)),
            pltpu.SemaphoreType.DMA((2, 3)),
            pltpu.SemaphoreType.DMA((count + 1,)),
            pltpu.SemaphoreType.REGULAR,
            pltpu.SemaphoreType.REGULAR,
        ],
        compiler_params=pltpu.CompilerParams(
            vmem_limit_bytes=56 << 20, collective_id=0, has_side_effects=True
        ),
        name="filter_and_gram",
    )(bounds, states, potential)


def times(left, right, left_dim, right_dim):
    return lax.dot_general(
        left,
        right,
        (((left_dim,), (right_dim,)), ((), ())),
        precision=lax.Precision.HIGHEST,
        preferred_element_type=jnp.float32,
    )


def inverse_factor(tiles, beside=None):
    row = lax.broadcasted_iota(jnp.int32, (8, 128), 0)
    lane = lax.broadcasted_iota(jnp.int32, (8, 128), 1)

    def of_row(value, index):
        return jnp.broadcast_to(value[index : index + 1, :], (8, 128))

    def of_lane(value, index):
        return jnp.broadcast_to(value[:, index : index + 1], (8, 128))

    tiles = list(tiles)
    result = []
    for tile in range(16):
        start = 8 * tile
        here = tiles[tile]
        solved = jnp.zeros((8, 128), jnp.float32)
        columns = [of_lane(here, start + c) for c in range(8)]
        below = range(tile + 1, 16)
        multipliers = [[of_lane(tiles[i], start + c) for c in range(8)] for i in below]
        inverses = []
        for i in range(8):
            pivot = of_row(columns[i], i)
            inverses.append(1.0 / pivot)
            here = jnp.where(lane == start + i, jnp.where(row == i, 1.0, 0.0), here)
            pivot_row = of_row(here, i)
            solved = jnp.where(row == i, pivot_row * lax.rsqrt(pivot), solved)
            others = jnp.where(row == i, 0.0, columns[i]) * inverses[i]
            here = here - others * pivot_row
            for c in range(i + 1, 8):
                columns[c] = columns[c] - others * of_row(columns[c], i)
        result.append(jnp.where(lane <= start + row, solved, 0.0))
        spread = [of_row(here, c) * inverses[c] for c in range(8)]
        for multiplier, i in zip(multipliers, below):
            parts = [multiplier[c] * spread[c] for c in range(8)]
            total = ((parts[0] + parts[1]) + (parts[2] + parts[3])) + (
                (parts[4] + parts[5]) + (parts[6] + parts[7])
            )
            tiles[i] = jnp.where((lane >= start) & (lane < start + 8), 0.0, tiles[i]) - total
        if beside is not None:
            beside(tile)
    return result


def solve_kernel(
    first_ref, low_ref, rest_ref, rows_ref, out_ref, second, rows, out, rows_sem, out_sem, *, scale
):
    half = first_ref.shape[0]
    width = rows_ref.shape[1]
    load = pltpu.make_async_copy(rows_ref, rows, rows_sem)
    load.start()
    first_piece = 16 - width // 128

    def beside(tile):
        if tile < first_piece:
            return
        if tile == first_piece:
            load.wait()
        here = pl.ds((tile - first_piece) * 128, 128)
        upper = times(first_ref[...], rows[0:half, here], 1, 0)
        out[0:half, here] = upper * scale
        rows[half:, here] = rows[half:, here] - times(low_ref[...], upper, 1, 0)

    tiles = inverse_factor([rest_ref[8 * i : 8 * i + 8] for i in range(16)], beside)
    upper_store = pltpu.make_async_copy(
        out.at[0:half], out_ref.at[0:half], out_sem.at[out_sem.shape[0] - 1]
    )
    upper_store.start()
    for i in range(16):
        second[8 * i : 8 * i + 8] = tiles[i] * scale
    pieces = out_sem.shape[0] - 1
    stores = [upper_store]
    for piece in range(pieces):
        here = pl.ds(piece * width // pieces, width // pieces)
        out[half:, here] = times(second[...], rows[half:, here], 1, 0)
        store = pltpu.make_async_copy(
            out.at[half:, here], out_ref.at[half:, here], out_sem.at[piece]
        )
        store.start()
        stores.append(store)
    for store in stores:
        store.wait()


def solve(first, low, rest, rows, scale):
    half = first.shape[0]
    return pl.pallas_call(
        functools.partial(solve_kernel, scale=scale),
        out_shape=jax.ShapeDtypeStruct(rows.shape, jnp.float32),
        in_specs=[pl.BlockSpec(memory_space=pltpu.VMEM)] * 3 + [pl.BlockSpec(memory_space=pl.ANY)],
        out_specs=pl.BlockSpec(memory_space=pl.ANY),
        scratch_shapes=[
            pltpu.VMEM((half, half), jnp.float32),
            pltpu.VMEM(rows.shape, jnp.float32),
            pltpu.VMEM(rows.shape, jnp.float32),
            pltpu.SemaphoreType.DMA,
            pltpu.SemaphoreType.DMA((4,)),
        ],
        compiler_params=pltpu.CompilerParams(vmem_limit_bytes=56 << 20),
        name="solve",
    )(first, low, rest, rows)


def per_device(initial_states, potential, bounds):
    row_block, first, low, rest = filter_and_gram(initial_states, potential, bounds)
    return solve(first, low, rest, row_block, math.sqrt(math.prod(initial_states.shape[1:])))


def solution(mesh):
    return jax.shard_map(
        per_device,
        mesh=mesh,
        in_specs=(P(("cuts", "state"), None, None, None), P(), P("cuts")),
        out_specs=P("cuts", "state"),
        check_vma=False,
    )
```

```python
import functools
import math

import jax
import jax.numpy as jnp
from jax import lax
from jax.experimental import pallas as pl
from jax.experimental.pallas import tpu as pltpu
from jax.sharding import PartitionSpec as P

DEGREE = 16
ANCHOR_VALUE = -1.125
XB = 8
GY = 128


def chebyshev_scalars(bounds_ref):
    low_end = jnp.full((8, GY), bounds_ref[0].astype(jnp.float32), jnp.float32) / 64.0
    high_end = jnp.full((8, GY), bounds_ref[1].astype(jnp.float32), jnp.float32) / 16.0
    half_width = (high_end - low_end) / 2.0
    centre = (high_end + low_end) / 2.0
    place = (ANCHOR_VALUE - centre) / half_width
    before, now = jnp.ones_like(place), place
    for _ in range(DEGREE - 1):
        before, now = now, 2.0 * place * now - before
    return half_width, centre, 1.0 / now


def circulant():
    row = lax.rem(lax.broadcasted_iota(jnp.int32, (2 * GY, GY), 0), GY)
    column = lax.broadcasted_iota(jnp.int32, (2 * GY, GY), 1)
    apart = lax.rem(row - column + GY, GY)
    near = jnp.where((apart == 1) | (apart == GY - 1), -16.0, 0.0)
    far = jnp.where((apart == 2) | (apart == GY - 2), 1.0, 0.0)
    return (near + far).astype(jnp.bfloat16)


def filter_step(source, target, diagonal, matrix, factor, scale):
    planes, rows = diagonal.shape[0], diagonal.shape[1]
    values = source[pl.ds(2, planes)].reshape(planes * rows * 8, GY)
    high = values.astype(jnp.bfloat16)
    low = (values - high.astype(jnp.float32)).astype(jnp.bfloat16)
    along_y = jnp.dot(
        jnp.concatenate([high, low], 1), matrix, preferred_element_type=jnp.float32
    ).reshape(planes, rows, 8, GY)
    for z in range(planes):
        here = [source[z + 2, r] for r in range(rows)]
        ring = (
            [pltpu.roll(here[r], 1, 0) for r in (rows - 2, rows - 1)]
            + here
            + [pltpu.roll(here[r], 7, 0) for r in (0, 1)]
        )
        for r in range(rows):
            near = (source[z + 1, r] + source[z + 3, r]) + (ring[r + 1] + ring[r + 3])
            far = (source[z, r] + source[z + 4, r]) + (ring[r] + ring[r + 4])
            total = far - 16.0 * near + diagonal[z, r] * here[r] + along_y[z, r]
            latest = factor * total - target[z + 2, r]
            if scale is not None:
                latest = latest * scale
            target[z + 2, r] = latest


GROUP = 4
PLANES_Z = 8
PLANE_XY = 16


def along(me, stride, extent, number):
    place = lax.rem(lax.div(me, stride), extent)
    return me + (lax.rem(place + number, extent) - place) * stride


def greet(semaphore, me, stride, extent):
    for number in range(1, extent):
        pl.semaphore_signal(
            semaphore,
            inc=1,
            device_id={"state": along(me, stride, extent, number)},
            device_id_type=pl.DeviceIdType.MESH,
        )


def remote(source, target, send, receive, peer):
    return pltpu.make_async_remote_copy(
        src_ref=source,
        dst_ref=target,
        send_sem=send,
        recv_sem=receive,
        device_id={"state": peer},
        device_id_type=pl.DeviceIdType.MESH,
    )


def wait_bytes(ref, semaphore):
    pltpu.make_async_copy(ref, ref, semaphore).wait()


def filter_gram_kernel(
    bounds_ref,
    states_ref,
    potential_ref,
    rows_ref,
    first_ref,
    low_ref,
    rest_ref,
    initial,
    potential,
    buffers,
    diagonal,
    start,
    outbox,
    inbox,
    block,
    partial_first,
    partial_rest,
    plane_first,
    plane_rest,
    column_first,
    column_rest,
    gathered_first,
    gathered_rest,
    send_sem,
    recv_sem,
    own_sem,
    rows_sem,
    sum_send,
    sum_recv,
    load_sem,
    lend_sem,
    heard_x,
    heard_y,
):
    partial, in_plane = (partial_first, partial_rest), (plane_first, plane_rest)
    in_column, gathered = (column_first, column_rest), (gathered_first, gathered_rest)
    states, planes, width, _ = states_ref.shape
    rows = width // 8
    devices = 128
    piece = planes * width // devices
    me = lax.axis_index("state")

    loads = [
        pltpu.make_async_copy(potential_ref, potential, load_sem.at[states]),
    ] + [
        pltpu.make_async_copy(states_ref.at[state], initial.at[state], load_sem.at[state])
        for state in range(states)
    ]
    for load in loads:
        load.start()

    barrier = pltpu.get_barrier_semaphore()
    greet(barrier, me, 16, 8)
    greet(barrier, me, 4, 4)
    greet(barrier, me, 1, 4)

    half_width, centre, last_scale = chebyshev_scalars(bounds_ref)
    shift = 3.75 - centre
    factor = 2.0 / (24.0 * half_width)
    zero = jnp.zeros((rows, 8, GY), jnp.float32)

    def load_potential(group, _):
        for part in range(GROUP):
            z = group * GROUP + part
            for r in range(rows):
                diagonal[z, r] = 24.0 * (potential[z, pl.ds(r, 8, stride=rows), :] + shift)
        return 0

    for buffer in range(2):
        for z in (0, 1, planes + 2, planes + 3):
            buffers[buffer, z] = zero
    loads[0].wait()
    lax.fori_loop(0, planes // GROUP, load_potential, 0)
    even, odd = buffers.at[0], buffers.at[1]
    matrix = circulant()
    toward = jnp.where(lax.axis_index("cuts") == 0, 1, -1)
    mine, level = lax.rem(me, PLANE_XY), lax.div(me, PLANE_XY)

    def at_level(number):
        return lax.rem(level + number + PLANES_Z, PLANES_Z) * PLANE_XY

    def to_float(state):
        def convert(group, _):
            for part in range(GROUP):
                z = group * GROUP + part
                start[state, z] = initial[state, z].astype(jnp.float32)
            return 0

        lax.fori_loop(0, planes // GROUP, convert, 0)

    lend = remote(start.at[1], start.at[2], lend_sem.at[0], lend_sem.at[1], at_level(toward) + mine)
    loads[1].wait()
    to_float(0)

    def one_turn(turn, _):
        @pl.when(turn == 2)
        def _():
            lend.wait()

        def load(group, _):
            for part in range(GROUP):
                z = group * GROUP + part
                for r in range(rows):
                    even[z + 2, r] = start[turn, z, pl.ds(r, 8, stride=rows), :]
                odd[z + 2] = zero
            return 0

        lax.fori_loop(0, planes // GROUP, load, 0)

        def two_steps(pair, _):
            first = jnp.where(pair == 0, 0.5 * factor, factor)
            filter_step(even, odd, diagonal, matrix, first, None)

            @pl.when((turn == 0) & (pair == 1))
            def _():
                pl.semaphore_wait(barrier, 7 + 3 + 3)
                greet(heard_x, me, 1, 4)
                loads[2].wait()
                to_float(1)
                lend.start()

            @pl.when((turn == 0) & (pair == 4))
            def _():
                pl.semaphore_wait(heard_x, 3)
                greet(heard_y, me, 4, 4)

            last = jnp.where(pair == DEGREE // 2 - 1, last_scale, 1.0)
            filter_step(odd, even, diagonal, matrix, factor, last)
            return 0

        lax.fori_loop(0, DEGREE // 2, two_steps, 0)

        def store(group, _):
            for part in range(GROUP):
                z = group * GROUP + part
                for r in range(rows):
                    outbox[pl.ds((turn * planes + z) * width + r, 8, stride=rows), :] = even[z + 2, r]
            return 0

        lax.fori_loop(0, planes // GROUP, store, 0)

        @pl.when(turn == 0)
        def _():
            pl.semaphore_wait(heard_y, 3)

        depth = jnp.where(turn == 0, PLANES_Z, PLANES_Z // 2)
        heading = jnp.where(turn == 1, -toward, toward)
        y, x = lax.div(mine, 4), lax.rem(mine, 4)

        def send_column(column, _):
            beside = lax.rem(y + lax.div(column, 4), 4) * 4 + lax.rem(x + lax.rem(column, 4), 4)

            def send(number, _):
                peer = at_level(number * heading) + beside
                remote(
                    outbox.at[pl.ds((turn * devices + peer) * piece, piece)],
                    inbox.at[pl.ds(inbox_row(turn), piece)],
                    send_sem,
                    recv_sem.at[jnp.minimum(turn, 1)],
                    peer,
                ).start()
                return 0

            lax.fori_loop(jnp.where(column == 0, 1, 0), depth, send, 0)
            return 0

        lax.fori_loop(0, PLANE_XY, send_column, 0)
        own_copy(turn).start()
        return 0

    def inbox_row(turn):
        owner = jnp.where(turn == 2, at_level(-toward) + mine, me)
        return (owner * states + jnp.minimum(turn, 1)) * piece

    def own_copy(turn):
        return pltpu.make_async_copy(
            outbox.at[pl.ds((turn * devices + me) * piece, piece)],
            inbox.at[pl.ds(inbox_row(turn), piece)],
            own_sem.at[turn],
        )

    lax.fori_loop(0, states + 1, one_turn, 0)
    for turn in range(states + 1):
        own_copy(turn).wait()
    wait_bytes(inbox.at[pl.ds(0, (devices - 1) * piece)], recv_sem.at[0])
    wait_bytes(inbox.at[pl.ds(0, (devices - 2) * piece)], recv_sem.at[1])
    wait_bytes(outbox.at[pl.ds(0, (2 * devices - 3) * piece)], send_sem)

    total = devices * states

    def gram_piece(column, _):
        here = inbox[pl.ds(column, total, stride=piece), :]
        block[:, pl.ds(pl.multiple_of(column * GY, GY), GY)] = here
        return 0

    lax.fori_loop(0, piece, gram_piece, 0)
    rows_copy = pltpu.make_async_copy(block, rows_ref, rows_sem)
    rows_copy.start()
    half = total // 2


    def part_of(ref, number):
        count = ref.shape[0] // PLANE_XY
        return pl.ds(pl.multiple_of(number * count, 8), count)

    def plane_peer(number):
        y, x = lax.div(mine, 4), lax.rem(mine, 4)
        return lax.rem(y + lax.div(number, 4), 4) * 4 + lax.rem(x + lax.rem(number, 4), 4)

    def first_round(which):
        source, target = partial[which], in_plane[which]

        def share(number, _):
            to = plane_peer(number)
            remote(
                source.at[part_of(source, to)],
                target.at[mine],
                sum_send.at[which, 0],
                sum_recv.at[which, 0],
                level * PLANE_XY + to,
            ).start()
            return 0

        lax.fori_loop(1, PLANE_XY, share, 0)
        target[mine] = source[part_of(source, mine), :]

    def total_of(ref):
        parts = [ref[number] for number in range(ref.shape[0])]
        while len(parts) > 1:
            parts = [parts[i] + parts[i + 1] for i in range(0, len(parts), 2)]
        return parts[0]

    def second_round(which):
        source, target = in_plane[which], in_column[which]
        wait_bytes(source.at[pl.ds(0, PLANE_XY - 1)], sum_recv.at[which, 0])
        target[level] = total_of(source)

        def along_z(number, _):
            remote(
                target.at[level],
                target.at[level],
                sum_send.at[which, 1],
                sum_recv.at[which, 1],
                lax.rem(level + number, PLANES_Z) * PLANE_XY + mine,
            ).start()
            return 0

        lax.fori_loop(1, PLANES_Z, along_z, 0)

    def third_round(which):
        source, target = in_column[which], gathered[which]
        wait_bytes(source.at[pl.ds(0, PLANES_Z - 1)], sum_recv.at[which, 1])
        here = part_of(target, mine)
        target[here, :] = total_of(source)

        def spread(number, _):
            remote(
                target.at[here],
                target.at[here],
                sum_send.at[which, 2],
                sum_recv.at[which, 2],
                level * PLANE_XY + plane_peer(number),
            ).start()
            return 0

        lax.fori_loop(1, PLANE_XY, spread, 0)

    def most_of(ref):
        return ref.at[pl.ds(0, ref.shape[0] // PLANE_XY * (PLANE_XY - 1))]

    partial[0][...] = times(block[0:half], block[0:half], 1, 1)
    first_round(0)
    partial[1][0:half] = times(block[half:], block[0:half], 1, 1)
    partial[1][half:] = times(block[half:], block[half:], 1, 1)
    first_round(1)
    second_round(0)
    second_round(1)
    third_round(0)
    third_round(1)
    wait_bytes(most_of(gathered[0]), sum_recv.at[0, 2])
    tiles = inverse_factor([gathered[0][8 * i : 8 * i + 8] for i in range(16)])
    for i in range(16):
        first_ref[8 * i : 8 * i + 8] = tiles[i]
    wait_bytes(most_of(gathered[1]), sum_recv.at[1, 2])
    low = times(gathered[1][0:half], first_ref[...], 1, 1)
    low_ref[...] = low
    rest_ref[...] = gathered[1][half:] - times(low, low, 1, 1)
    for which in range(2):
        wait_bytes(in_plane[which].at[pl.ds(0, PLANE_XY - 1)], sum_send.at[which, 0])
        wait_bytes(in_column[which].at[pl.ds(0, PLANES_Z - 1)], sum_send.at[which, 1])
        wait_bytes(most_of(gathered[which]), sum_send.at[which, 2])
    rows_copy.wait()


def filter_and_gram(states, potential, bounds):
    count, planes, width = states.shape[:3]
    total, half = count * 128, count * 64
    points = planes * width * GY // 128
    return pl.pallas_call(
        filter_gram_kernel,
        out_shape=[
            jax.ShapeDtypeStruct((total, points), jnp.float32),
            jax.ShapeDtypeStruct((half, half), jnp.float32),
            jax.ShapeDtypeStruct((half, half), jnp.float32),
            jax.ShapeDtypeStruct((half, half), jnp.float32),
        ],
        in_specs=[
            pl.BlockSpec(memory_space=pltpu.SMEM),
            pl.BlockSpec(memory_space=pl.ANY),
            pl.BlockSpec(memory_space=pl.ANY),
        ],
        out_specs=[pl.BlockSpec(memory_space=pl.ANY)] + [pl.BlockSpec(memory_space=pltpu.VMEM)] * 3,
        scratch_shapes=[
            pltpu.VMEM(states.shape, states.dtype),
            pltpu.VMEM(potential.shape, potential.dtype),
            pltpu.VMEM((2, planes + 4, width // 8, 8, GY), jnp.float32),
            pltpu.VMEM((planes, width // 8, 8, GY), jnp.float32),
            pltpu.VMEM((count + 1, planes, width, GY), jnp.float32),
            pltpu.VMEM(((count + 1) * planes * width, GY), jnp.float32),
            pltpu.VMEM((count * planes * width, GY), jnp.float32),
            pltpu.VMEM((total, points), jnp.float32),
            pltpu.VMEM((half, GY), jnp.float32),
            pltpu.VMEM((total, GY), jnp.float32),
            pltpu.VMEM((PLANE_XY, half // PLANE_XY, GY), jnp.float32),
            pltpu.VMEM((PLANE_XY, total // PLANE_XY, GY), jnp.float32),
            pltpu.VMEM((PLANES_Z, half // PLANE_XY, GY), jnp.float32),
            pltpu.VMEM((PLANES_Z, total // PLANE_XY, GY), jnp.float32),
            pltpu.VMEM((half, GY), jnp.float32),
            pltpu.VMEM((total, GY), jnp.float32),
            pltpu.SemaphoreType.DMA,
            pltpu.SemaphoreType.DMA((2,)),
            pltpu.SemaphoreType.DMA((count + 1,)),
            pltpu.SemaphoreType.DMA,
            pltpu.SemaphoreType.DMA((2, 3)),
            pltpu.SemaphoreType.DMA((2, 3)),
            pltpu.SemaphoreType.DMA((count + 1,)),
            pltpu.SemaphoreType.DMA((2,)),
            pltpu.SemaphoreType.REGULAR,
            pltpu.SemaphoreType.REGULAR,
        ],
        compiler_params=pltpu.CompilerParams(
            vmem_limit_bytes=56 << 20, collective_id=0, has_side_effects=True
        ),
        name="filter_and_gram",
    )(bounds, states, potential)


def times(left, right, left_dim, right_dim):
    return lax.dot_general(
        left,
        right,
        (((left_dim,), (right_dim,)), ((), ())),
        precision=lax.Precision.HIGHEST,
        preferred_element_type=jnp.float32,
    )


def inverse_factor(tiles, beside=None):
    row = lax.broadcasted_iota(jnp.int32, (8, 128), 0)
    lane = lax.broadcasted_iota(jnp.int32, (8, 128), 1)

    def of_row(value, index):
        return jnp.broadcast_to(value[index : index + 1, :], (8, 128))

    def of_lane(value, index):
        return jnp.broadcast_to(value[:, index : index + 1], (8, 128))

    tiles = list(tiles)
    result = []
    for tile in range(16):
        start = 8 * tile
        here = tiles[tile]
        solved = jnp.zeros((8, 128), jnp.float32)
        columns = [of_lane(here, start + c) for c in range(8)]
        below = range(tile + 1, 16)
        multipliers = [[of_lane(tiles[i], start + c) for c in range(8)] for i in below]
        inverses = []
        for i in range(8):
            pivot = of_row(columns[i], i)
            inverses.append(1.0 / pivot)
            here = jnp.where(lane == start + i, jnp.where(row == i, 1.0, 0.0), here)
            pivot_row = of_row(here, i)
            solved = jnp.where(row == i, pivot_row * lax.rsqrt(pivot), solved)
            others = jnp.where(row == i, 0.0, columns[i]) * inverses[i]
            here = here - others * pivot_row
            for c in range(i + 1, 8):
                columns[c] = columns[c] - others * of_row(columns[c], i)
        result.append(jnp.where(lane <= start + row, solved, 0.0))
        spread = [of_row(here, c) * inverses[c] for c in range(8)]
        for multiplier, i in zip(multipliers, below):
            parts = [multiplier[c] * spread[c] for c in range(8)]
            total = ((parts[0] + parts[1]) + (parts[2] + parts[3])) + (
                (parts[4] + parts[5]) + (parts[6] + parts[7])
            )
            tiles[i] = jnp.where((lane >= start) & (lane < start + 8), 0.0, tiles[i]) - total
        if beside is not None:
            beside(tile)
    return result


def solve_kernel(
    first_ref, low_ref, rest_ref, rows_ref, out_ref, second, rows, out, rows_sem, out_sem, *, scale
):
    half = first_ref.shape[0]
    width = rows_ref.shape[1]
    load = pltpu.make_async_copy(rows_ref, rows, rows_sem)
    load.start()
    first_piece = 16 - width // 128

    def beside(tile):
        if tile < first_piece:
            return
        if tile == first_piece:
            load.wait()
        here = pl.ds((tile - first_piece) * 128, 128)
        upper = times(first_ref[...], rows[0:half, here], 1, 0)
        out[0:half, here] = upper * scale
        rows[half:, here] = rows[half:, here] - times(low_ref[...], upper, 1, 0)

    tiles = inverse_factor([rest_ref[8 * i : 8 * i + 8] for i in range(16)], beside)
    upper_store = pltpu.make_async_copy(
        out.at[0:half], out_ref.at[0:half], out_sem.at[out_sem.shape[0] - 1]
    )
    upper_store.start()
    for i in range(16):
        second[8 * i : 8 * i + 8] = tiles[i] * scale
    pieces = out_sem.shape[0] - 1
    stores = [upper_store]
    for piece in range(pieces):
        here = pl.ds(piece * width // pieces, width // pieces)
        out[half:, here] = times(second[...], rows[half:, here], 1, 0)
        store = pltpu.make_async_copy(
            out.at[half:, here], out_ref.at[half:, here], out_sem.at[piece]
        )
        store.start()
        stores.append(store)
    for store in stores:
        store.wait()


def solve(first, low, rest, rows, scale):
    half = first.shape[0]
    return pl.pallas_call(
        functools.partial(solve_kernel, scale=scale),
        out_shape=jax.ShapeDtypeStruct(rows.shape, jnp.float32),
        in_specs=[pl.BlockSpec(memory_space=pltpu.VMEM)] * 3 + [pl.BlockSpec(memory_space=pl.ANY)],
        out_specs=pl.BlockSpec(memory_space=pl.ANY),
        scratch_shapes=[
            pltpu.VMEM((half, half), jnp.float32),
            pltpu.VMEM(rows.shape, jnp.float32),
            pltpu.VMEM(rows.shape, jnp.float32),
            pltpu.SemaphoreType.DMA,
            pltpu.SemaphoreType.DMA((4,)),
        ],
        compiler_params=pltpu.CompilerParams(vmem_limit_bytes=56 << 20),
        name="solve",
    )(first, low, rest, rows)


def per_device(initial_states, potential, bounds):
    row_block, first, low, rest = filter_and_gram(initial_states, potential, bounds)
    return solve(first, low, rest, row_block, math.sqrt(math.prod(initial_states.shape[1:])))


def solution(mesh):
    return jax.shard_map(
        per_device,
        mesh=mesh,
        in_specs=(P(("cuts", "state"), None, None, None), P(), P("cuts")),
        out_specs=P("cuts", "state"),
        check_vma=False,
    )
```

```python
import functools
import math

import jax
import jax.numpy as jnp
from jax import lax
from jax.experimental import pallas as pl
from jax.experimental.pallas import tpu as pltpu
from jax.sharding import PartitionSpec as P

DEGREE = 16
ANCHOR_VALUE = -1.125
XB = 8
GY = 128


def chebyshev_scalars(bounds_ref):
    low_end = jnp.full((8, GY), bounds_ref[0].astype(jnp.float32), jnp.float32) / 64.0
    high_end = jnp.full((8, GY), bounds_ref[1].astype(jnp.float32), jnp.float32) / 16.0
    half_width = (high_end - low_end) / 2.0
    centre = (high_end + low_end) / 2.0
    place = (ANCHOR_VALUE - centre) / half_width
    before, now = jnp.ones_like(place), place
    for _ in range(DEGREE - 1):
        before, now = now, 2.0 * place * now - before
    return half_width, centre, 1.0 / now


def circulant():
    row = lax.broadcasted_iota(jnp.int32, (2 * GY, GY), 0)
    column = lax.broadcasted_iota(jnp.int32, (2 * GY, GY), 1)
    apart = jnp.bitwise_and(row - column, GY - 1)
    near = jnp.where((apart == 1) | (apart == GY - 1), -16.0, 0.0)
    far = jnp.where((apart == 2) | (apart == GY - 2), 1.0, 0.0)
    return (near + far).astype(jnp.bfloat16)


def filter_step(source, target, diagonal, matrix, factor, finish=None):
    planes, rows = diagonal.shape[0], diagonal.shape[1]
    values = source[pl.ds(2, planes)].reshape(planes * rows * 8, GY)
    high = values.astype(jnp.bfloat16)
    low = (values - high.astype(jnp.float32)).astype(jnp.bfloat16)
    along_y = jnp.dot(
        jnp.concatenate([high, low], 1), matrix, preferred_element_type=jnp.float32
    ).reshape(planes, rows, 8, GY)
    for z in range(planes):
        here = [source[z + 2, r] for r in range(rows)]
        ring = (
            [pltpu.roll(here[r], 1, 0) for r in (rows - 2, rows - 1)]
            + here
            + [pltpu.roll(here[r], 7, 0) for r in (0, 1)]
        )
        for r in range(rows):
            near = (source[z + 1, r] + source[z + 3, r]) + (ring[r + 1] + ring[r + 3])
            far = (source[z, r] + source[z + 4, r]) + (ring[r] + ring[r + 4])
            total = far - 16.0 * near + diagonal[z, r] * here[r] + along_y[z, r]
            latest = factor * total - target[z + 2, r]
            if finish is None:
                target[z + 2, r] = latest
            else:
                finish(z, r, latest)


GROUP = 8
PLANES_Z = 8
PLANE_XY = 16


def along(me, stride, extent, number):
    place = lax.rem(lax.div(me, stride), extent)
    return me + (lax.rem(place + number, extent) - place) * stride


def greet(semaphore, me, stride, extent):
    for number in range(1, extent):
        pl.semaphore_signal(
            semaphore,
            inc=1,
            device_id={"state": along(me, stride, extent, number)},
            device_id_type=pl.DeviceIdType.MESH,
        )


def remote(source, target, send, receive, peer):
    return pltpu.make_async_remote_copy(
        src_ref=source,
        dst_ref=target,
        send_sem=send,
        recv_sem=receive,
        device_id={"state": peer},
        device_id_type=pl.DeviceIdType.MESH,
    )


def wait_bytes(ref, semaphore):
    pltpu.make_async_copy(ref, ref, semaphore).wait()


def filter_gram_kernel(
    bounds_ref,
    states_ref,
    potential_ref,
    rows_ref,
    first_ref,
    low_ref,
    rest_ref,
    initial,
    potential,
    buffers,
    diagonal,
    start,
    outbox,
    inbox,
    block,
    partial_first,
    partial_rest,
    plane_first,
    plane_rest,
    column_first,
    column_rest,
    gathered_first,
    gathered_rest,
    send_sem,
    recv_sem,
    own_sem,
    rows_sem,
    sum_send,
    sum_recv,
    load_sem,
    lend_sem,
    heard_x,
    heard_y,
):
    partial, in_plane = (partial_first, partial_rest), (plane_first, plane_rest)
    in_column, gathered = (column_first, column_rest), (gathered_first, gathered_rest)
    states, planes, width, _ = states_ref.shape
    rows = width // 8
    devices = 128
    piece = planes * width // devices
    me = lax.axis_index("state")

    pieces = planes // GROUP
    loads = []
    for number, (source, target) in enumerate(
        [(potential_ref, potential)]
        + [(states_ref.at[state], initial.at[state]) for state in range(states)]
    ):
        here = [pl.ds(piece * GROUP, GROUP) for piece in range(pieces)]
        loads.append(
            [
                pltpu.make_async_copy(source.at[here[i]], target.at[here[i]], load_sem.at[number, i])
                for i in range(pieces)
            ]
        )
        for load in loads[number]:
            load.start()

    barrier = pltpu.get_barrier_semaphore()
    greet(barrier, me, 16, 8)
    greet(barrier, me, 4, 4)
    greet(barrier, me, 1, 4)

    half_width, centre, last_scale = chebyshev_scalars(bounds_ref)
    shift = 3.75 - centre
    factor = 2.0 / (24.0 * half_width)
    zero = jnp.zeros((rows, 8, GY), jnp.float32)

    def load_potential(group, _):
        for part in range(GROUP):
            z = group * GROUP + part
            for r in range(rows):
                diagonal[z, r] = 24.0 * (potential[z, pl.ds(r, 8, stride=rows), :] + shift)
        return 0

    for buffer in range(2):
        for z in (0, 1, planes + 2, planes + 3):
            buffers[buffer, z] = zero
    even, odd = buffers.at[0], buffers.at[1]
    matrix = circulant()
    for load in loads[0]:
        load.wait()
    lax.fori_loop(0, planes // GROUP, load_potential, 0)
    toward = jnp.where(lax.axis_index("cuts") == 0, 1, -1)
    mine, level = lax.rem(me, PLANE_XY), lax.div(me, PLANE_XY)

    def at_level(number):
        return lax.rem(level + number + PLANES_Z, PLANES_Z) * PLANE_XY

    def to_float(state):
        def convert(group, _):
            for part in range(GROUP):
                z = group * GROUP + part
                start[state, z] = initial[state, z].astype(jnp.float32)
            return 0

        lax.fori_loop(0, planes // GROUP, convert, 0)

    lend = remote(start.at[1], start.at[2], lend_sem.at[0], lend_sem.at[1], at_level(toward) + mine)
    for load in loads[1]:
        load.wait()
    to_float(0)

    def one_turn(turn, _):
        @pl.when(turn == 2)
        def _():
            lend.wait()

        def load(group, _):
            for part in range(GROUP):
                z = group * GROUP + part
                for r in range(rows):
                    even[z + 2, r] = start[turn, z, pl.ds(r, 8, stride=rows), :]
                odd[z + 2] = zero
            return 0

        lax.fori_loop(0, planes // GROUP, load, 0)

        def two_steps(pair, _):
            first = jnp.where(pair == 0, 0.5 * factor, factor)
            filter_step(even, odd, diagonal, matrix, first)

            @pl.when((turn == 0) & (pair == 0))
            def _():
                pl.semaphore_wait(barrier, 7 + 3 + 3)
                greet(heard_x, me, 1, 4)
                for load in loads[2]:
                    load.wait()
                to_float(1)
                lend.start()

            @pl.when((turn == 0) & (pair == 3))
            def _():
                pl.semaphore_wait(heard_x, 3)
                greet(heard_y, me, 4, 4)

            filter_step(odd, even, diagonal, matrix, factor)
            return 0

        lax.fori_loop(0, DEGREE // 2 - 1, two_steps, 0)
        filter_step(even, odd, diagonal, matrix, factor)

        def finish(z, r, latest):
            outbox[pl.ds((turn * planes + z) * width + r, 8, stride=rows), :] = latest * last_scale

        filter_step(odd, even, diagonal, matrix, factor, finish)

        @pl.when(turn == 0)
        def _():
            pl.semaphore_wait(heard_y, 3)

        depth = jnp.where(turn == 0, PLANES_Z, PLANES_Z // 2)
        heading = jnp.where(turn == 1, -toward, toward)
        y, x = lax.div(mine, 4), lax.rem(mine, 4)

        def send_column(column, _):
            beside = lax.rem(y + lax.div(column, 4), 4) * 4 + lax.rem(x + lax.rem(column, 4), 4)

            def send(number, _):
                peer = at_level(number * heading) + beside
                remote(
                    outbox.at[pl.ds((turn * devices + peer) * piece, piece)],
                    inbox.at[pl.ds(inbox_row(turn), piece)],
                    send_sem,
                    recv_sem.at[jnp.minimum(turn, 1)],
                    peer,
                ).start()
                return 0

            lax.fori_loop(jnp.where(column == 0, 1, 0), depth, send, 0)
            return 0

        lax.fori_loop(0, PLANE_XY, send_column, 0)
        own_copy(turn).start()
        return 0

    def inbox_row(turn):
        owner = jnp.where(turn == 2, at_level(-toward) + mine, me)
        return (owner * states + jnp.minimum(turn, 1)) * piece

    def own_copy(turn):
        return pltpu.make_async_copy(
            outbox.at[pl.ds((turn * devices + me) * piece, piece)],
            inbox.at[pl.ds(inbox_row(turn), piece)],
            own_sem.at[turn],
        )

    lax.fori_loop(0, states + 1, one_turn, 0)
    for turn in range(states + 1):
        own_copy(turn).wait()
    wait_bytes(inbox.at[pl.ds(0, (devices - 1) * piece)], recv_sem.at[0])
    wait_bytes(inbox.at[pl.ds(0, (devices - 2) * piece)], recv_sem.at[1])
    wait_bytes(outbox.at[pl.ds(0, (2 * devices - 3) * piece)], send_sem)

    total = devices * states

    def gram_piece(column, _):
        here = inbox[pl.ds(column, total, stride=piece), :]
        block[:, pl.ds(pl.multiple_of(column * GY, GY), GY)] = here
        return 0

    lax.fori_loop(0, piece, gram_piece, 0)
    rows_copy = pltpu.make_async_copy(block, rows_ref, rows_sem)
    rows_copy.start()
    half = total // 2


    def part_of(ref, number):
        count = ref.shape[0] // PLANE_XY
        return pl.ds(pl.multiple_of(number * count, 8), count)

    def plane_peer(number):
        y, x = lax.div(mine, 4), lax.rem(mine, 4)
        return lax.rem(y + lax.div(number, 4), 4) * 4 + lax.rem(x + lax.rem(number, 4), 4)

    def first_round(which):
        source, target = partial[which], in_plane[which]

        def share(number, _):
            to = plane_peer(number)
            remote(
                source.at[part_of(source, to)],
                target.at[mine],
                sum_send.at[which, 0],
                sum_recv.at[which, 0],
                level * PLANE_XY + to,
            ).start()
            return 0

        lax.fori_loop(1, PLANE_XY, share, 0)
        target[mine] = source[part_of(source, mine), :]

    def total_of(ref):
        parts = [ref[number] for number in range(ref.shape[0])]
        while len(parts) > 1:
            parts = [parts[i] + parts[i + 1] for i in range(0, len(parts), 2)]
        return parts[0]

    def second_round(which):
        source, target = in_plane[which], in_column[which]
        wait_bytes(source.at[pl.ds(0, PLANE_XY - 1)], sum_recv.at[which, 0])
        target[level] = total_of(source)

        def along_z(number, _):
            remote(
                target.at[level],
                target.at[level],
                sum_send.at[which, 1],
                sum_recv.at[which, 1],
                lax.rem(level + number, PLANES_Z) * PLANE_XY + mine,
            ).start()
            return 0

        lax.fori_loop(1, PLANES_Z, along_z, 0)

    def third_round(which):
        source, target = in_column[which], gathered[which]
        wait_bytes(source.at[pl.ds(0, PLANES_Z - 1)], sum_recv.at[which, 1])
        here = part_of(target, mine)
        target[here, :] = total_of(source)

        def spread(number, _):
            remote(
                target.at[here],
                target.at[here],
                sum_send.at[which, 2],
                sum_recv.at[which, 2],
                level * PLANE_XY + plane_peer(number),
            ).start()
            return 0

        lax.fori_loop(1, PLANE_XY, spread, 0)

    def most_of(ref):
        return ref.at[pl.ds(0, ref.shape[0] // PLANE_XY * (PLANE_XY - 1))]

    partial[0][...] = times(block[0:half], block[0:half], 1, 1)
    first_round(0)
    partial[1][0:half] = times(block[half:], block[0:half], 1, 1)
    partial[1][half:] = times(block[half:], block[half:], 1, 1)
    first_round(1)
    second_round(0)
    second_round(1)
    third_round(0)
    third_round(1)
    wait_bytes(most_of(gathered[0]), sum_recv.at[0, 2])
    tiles = inverse_factor([gathered[0][8 * i : 8 * i + 8] for i in range(16)])
    for i in range(16):
        first_ref[8 * i : 8 * i + 8] = tiles[i]
    wait_bytes(most_of(gathered[1]), sum_recv.at[1, 2])
    low = times(gathered[1][0:half], first_ref[...], 1, 1)
    low_ref[...] = low
    rest_ref[...] = gathered[1][half:] - times(low, low, 1, 1)
    for which in range(2):
        wait_bytes(in_plane[which].at[pl.ds(0, PLANE_XY - 1)], sum_send.at[which, 0])
        wait_bytes(in_column[which].at[pl.ds(0, PLANES_Z - 1)], sum_send.at[which, 1])
        wait_bytes(most_of(gathered[which]), sum_send.at[which, 2])
    rows_copy.wait()


def filter_and_gram(states, potential, bounds):
    count, planes, width = states.shape[:3]
    total, half = count * 128, count * 64
    points = planes * width * GY // 128
    return pl.pallas_call(
        filter_gram_kernel,
        out_shape=[
            jax.ShapeDtypeStruct((total, points), jnp.float32),
            jax.ShapeDtypeStruct((half, half), jnp.float32),
            jax.ShapeDtypeStruct((half, half), jnp.float32),
            jax.ShapeDtypeStruct((half, half), jnp.float32),
        ],
        in_specs=[
            pl.BlockSpec(memory_space=pltpu.SMEM),
            pl.BlockSpec(memory_space=pl.ANY),
            pl.BlockSpec(memory_space=pl.ANY),
        ],
        out_specs=[pl.BlockSpec(memory_space=pl.ANY)] + [pl.BlockSpec(memory_space=pltpu.VMEM)] * 3,
        scratch_shapes=[
            pltpu.VMEM(states.shape, states.dtype),
            pltpu.VMEM(potential.shape, potential.dtype),
            pltpu.VMEM((2, planes + 4, width // 8, 8, GY), jnp.float32),
            pltpu.VMEM((planes, width // 8, 8, GY), jnp.float32),
            pltpu.VMEM((count + 1, planes, width, GY), jnp.float32),
            pltpu.VMEM(((count + 1) * planes * width, GY), jnp.float32),
            pltpu.VMEM((count * planes * width, GY), jnp.float32),
            pltpu.VMEM((total, points), jnp.float32),
            pltpu.VMEM((half, GY), jnp.float32),
            pltpu.VMEM((total, GY), jnp.float32),
            pltpu.VMEM((PLANE_XY, half // PLANE_XY, GY), jnp.float32),
            pltpu.VMEM((PLANE_XY, total // PLANE_XY, GY), jnp.float32),
            pltpu.VMEM((PLANES_Z, half // PLANE_XY, GY), jnp.float32),
            pltpu.VMEM((PLANES_Z, total // PLANE_XY, GY), jnp.float32),
            pltpu.VMEM((half, GY), jnp.float32),
            pltpu.VMEM((total, GY), jnp.float32),
            pltpu.SemaphoreType.DMA,
            pltpu.SemaphoreType.DMA((2,)),
            pltpu.SemaphoreType.DMA((count + 1,)),
            pltpu.SemaphoreType.DMA,
            pltpu.SemaphoreType.DMA((2, 3)),
            pltpu.SemaphoreType.DMA((2, 3)),
            pltpu.SemaphoreType.DMA((count + 1, planes // GROUP)),
            pltpu.SemaphoreType.DMA((2,)),
            pltpu.SemaphoreType.REGULAR,
            pltpu.SemaphoreType.REGULAR,
        ],
        compiler_params=pltpu.CompilerParams(
            vmem_limit_bytes=56 << 20, collective_id=0, has_side_effects=True
        ),
        name="filter_and_gram",
    )(bounds, states, potential)


def times(left, right, left_dim, right_dim):
    return lax.dot_general(
        left,
        right,
        (((left_dim,), (right_dim,)), ((), ())),
        precision=lax.Precision.HIGHEST,
        preferred_element_type=jnp.float32,
    )


def inverse_factor(tiles, beside=None):
    row = lax.broadcasted_iota(jnp.int32, (8, 128), 0)
    lane = lax.broadcasted_iota(jnp.int32, (8, 128), 1)

    def of_row(value, index):
        return jnp.broadcast_to(value[index : index + 1, :], (8, 128))

    def of_lane(value, index):
        return jnp.broadcast_to(value[:, index : index + 1], (8, 128))

    tiles = list(tiles)
    result = []
    for tile in range(16):
        start = 8 * tile
        here = tiles[tile]
        solved = jnp.zeros((8, 128), jnp.float32)
        columns = [of_lane(here, start + c) for c in range(8)]
        below = range(tile + 1, 16)
        multipliers = [[of_lane(tiles[i], start + c) for c in range(8)] for i in below]
        inverses = []
        for i in range(8):
            pivot = of_row(columns[i], i)
            inverses.append(1.0 / pivot)
            here = jnp.where(lane == start + i, jnp.where(row == i, 1.0, 0.0), here)
            pivot_row = of_row(here, i)
            solved = jnp.where(row == i, pivot_row * lax.rsqrt(pivot), solved)
            others = jnp.where(row == i, 0.0, columns[i]) * inverses[i]
            here = here - others * pivot_row
            for c in range(i + 1, 8):
                columns[c] = columns[c] - others * of_row(columns[c], i)
        result.append(jnp.where(lane <= start + row, solved, 0.0))
        spread = [of_row(here, c) * inverses[c] for c in range(8)]
        for multiplier, i in zip(multipliers, below):
            parts = [multiplier[c] * spread[c] for c in range(8)]
            total = ((parts[0] + parts[1]) + (parts[2] + parts[3])) + (
                (parts[4] + parts[5]) + (parts[6] + parts[7])
            )
            tiles[i] = jnp.where((lane >= start) & (lane < start + 8), 0.0, tiles[i]) - total
        if beside is not None:
            beside(tile)
    return result


def solve_kernel(
    first_ref, low_ref, rest_ref, rows_ref, out_ref, second, rows, out, rows_sem, out_sem, *, scale
):
    half = first_ref.shape[0]
    width = rows_ref.shape[1]
    loads = []
    for number in range(rows_sem.shape[0]):
        here = pl.ds(number * width // rows_sem.shape[0], width // rows_sem.shape[0])
        loads.append(pltpu.make_async_copy(rows_ref.at[:, here], rows.at[:, here], rows_sem.at[number]))
        loads[number].start()
    first_piece = 16 - width // 128
    per_load = width // 128 // len(loads)

    def beside(tile):
        if tile < first_piece:
            return
        if (tile - first_piece) % per_load == 0:
            loads[(tile - first_piece) // per_load].wait()
        here = pl.ds((tile - first_piece) * 128, 128)
        upper = times(first_ref[...], rows[0:half, here], 1, 0)
        out[0:half, here] = upper * scale
        rows[half:, here] = rows[half:, here] - times(low_ref[...], upper, 1, 0)

    tiles = inverse_factor([rest_ref[8 * i : 8 * i + 8] for i in range(16)], beside)
    upper_store = pltpu.make_async_copy(
        out.at[0:half], out_ref.at[0:half], out_sem.at[out_sem.shape[0] - 1]
    )
    upper_store.start()
    for i in range(16):
        second[8 * i : 8 * i + 8] = tiles[i] * scale
    pieces = out_sem.shape[0] - 1
    stores = [upper_store]
    for piece in range(pieces):
        here = pl.ds(piece * width // pieces, width // pieces)
        out[half:, here] = times(second[...], rows[half:, here], 1, 0)
        store = pltpu.make_async_copy(
            out.at[half:, here], out_ref.at[half:, here], out_sem.at[piece]
        )
        store.start()
        stores.append(store)
    for store in stores:
        store.wait()


def solve(first, low, rest, rows, scale):
    half = first.shape[0]
    return pl.pallas_call(
        functools.partial(solve_kernel, scale=scale),
        out_shape=jax.ShapeDtypeStruct(rows.shape, jnp.float32),
        in_specs=[pl.BlockSpec(memory_space=pltpu.VMEM)] * 3 + [pl.BlockSpec(memory_space=pl.ANY)],
        out_specs=pl.BlockSpec(memory_space=pl.ANY),
        scratch_shapes=[
            pltpu.VMEM((half, half), jnp.float32),
            pltpu.VMEM(rows.shape, jnp.float32),
            pltpu.VMEM(rows.shape, jnp.float32),
            pltpu.SemaphoreType.DMA((4,)),
            pltpu.SemaphoreType.DMA((4,)),
        ],
        compiler_params=pltpu.CompilerParams(vmem_limit_bytes=56 << 20),
        name="solve",
    )(first, low, rest, rows)


def per_device(initial_states, potential, bounds):
    row_block, first, low, rest = filter_and_gram(initial_states, potential, bounds)
    return solve(first, low, rest, row_block, math.sqrt(math.prod(initial_states.shape[1:])))


def solution(mesh):
    return jax.shard_map(
        per_device,
        mesh=mesh,
        in_specs=(P(("cuts", "state"), None, None, None), P(), P("cuts")),
        out_specs=P("cuts", "state"),
        check_vma=False,
    )
```

```python
import functools
import math

import jax
import jax.numpy as jnp
from jax import lax
from jax.experimental import pallas as pl
from jax.experimental.pallas import tpu as pltpu
from jax.sharding import PartitionSpec as P

DEGREE = 16
ANCHOR_VALUE = -1.125
XB = 8
GY = 128


def chebyshev_scalars(bounds_ref):
    low_end = jnp.full((8, GY), bounds_ref[0].astype(jnp.float32), jnp.float32) / 64.0
    high_end = jnp.full((8, GY), bounds_ref[1].astype(jnp.float32), jnp.float32) / 16.0
    half_width = (high_end - low_end) / 2.0
    centre = (high_end + low_end) / 2.0
    place = (ANCHOR_VALUE - centre) / half_width
    before, now = jnp.ones_like(place), place
    for _ in range(DEGREE - 1):
        before, now = now, 2.0 * place * now - before
    return half_width, centre, 1.0 / now


def circulant():
    row = lax.broadcasted_iota(jnp.int32, (2 * GY, GY), 0)
    column = lax.broadcasted_iota(jnp.int32, (2 * GY, GY), 1)
    apart = jnp.bitwise_and(row - column, GY - 1)
    near = jnp.where((apart == 1) | (apart == GY - 1), -16.0, 0.0)
    far = jnp.where((apart == 2) | (apart == GY - 2), 1.0, 0.0)
    return (near + far).astype(jnp.bfloat16)


def filter_step(source, target, diagonal, matrix, factor, finish=None):
    planes, rows = diagonal.shape[0], diagonal.shape[1]
    values = source[pl.ds(2, planes)].reshape(planes * rows * 8, GY)
    high = values.astype(jnp.bfloat16)
    low = (values - high.astype(jnp.float32)).astype(jnp.bfloat16)
    along_y = jnp.dot(
        jnp.concatenate([high, low], 1), matrix, preferred_element_type=jnp.float32
    ).reshape(planes, rows, 8, GY)
    for z in range(planes):
        here = [source[z + 2, r] for r in range(rows)]
        ring = (
            [pltpu.roll(here[r], 1, 0) for r in (rows - 2, rows - 1)]
            + here
            + [pltpu.roll(here[r], 7, 0) for r in (0, 1)]
        )
        for r in range(rows):
            near = (source[z + 1, r] + source[z + 3, r]) + (ring[r + 1] + ring[r + 3])
            far = (source[z, r] + source[z + 4, r]) + (ring[r] + ring[r + 4])
            total = far - 16.0 * near + diagonal[z, r] * here[r] + along_y[z, r]
            latest = factor * total - target[z + 2, r]
            if finish is None:
                target[z + 2, r] = latest
            else:
                finish(z, r, latest)


GROUP = 8
PLANES_Z = 8
PLANE_XY = 16


def along(me, stride, extent, number):
    place = lax.rem(lax.div(me, stride), extent)
    return me + (lax.rem(place + number, extent) - place) * stride


def greet(semaphore, me, stride, extent):
    for number in range(1, extent):
        pl.semaphore_signal(
            semaphore,
            inc=1,
            device_id={"state": along(me, stride, extent, number)},
            device_id_type=pl.DeviceIdType.MESH,
        )


def remote(source, target, send, receive, peer):
    return pltpu.make_async_remote_copy(
        src_ref=source,
        dst_ref=target,
        send_sem=send,
        recv_sem=receive,
        device_id={"state": peer},
        device_id_type=pl.DeviceIdType.MESH,
    )


def wait_bytes(ref, semaphore):
    pltpu.make_async_copy(ref, ref, semaphore).wait()


def filter_gram_kernel(
    bounds_ref,
    states_ref,
    potential_ref,
    rows_ref,
    first_ref,
    low_ref,
    rest_ref,
    initial,
    potential,
    buffers,
    diagonal,
    start,
    outbox,
    inbox,
    block,
    partial_first,
    partial_rest,
    plane_first,
    plane_rest,
    column_first,
    column_rest,
    gathered_first,
    gathered_rest,
    send_sem,
    recv_sem,
    own_sem,
    rows_sem,
    sum_send,
    sum_recv,
    load_sem,
    lend_sem,
    heard_x,
    heard_y,
):
    partial, in_plane = (partial_first, partial_rest), (plane_first, plane_rest)
    in_column, gathered = (column_first, column_rest), (gathered_first, gathered_rest)
    states, planes, width, _ = states_ref.shape
    rows = width // 8
    devices = 128
    piece = planes * width // devices
    me = lax.axis_index("state")

    pieces = planes // GROUP
    loads = []
    for number, (source, target) in enumerate(
        [(potential_ref, potential)]
        + [(states_ref.at[state], initial.at[state]) for state in range(states)]
    ):
        here = [pl.ds(piece * GROUP, GROUP) for piece in range(pieces)]
        loads.append(
            [
                pltpu.make_async_copy(source.at[here[i]], target.at[here[i]], load_sem.at[number, i])
                for i in range(pieces)
            ]
        )
        for load in loads[number]:
            load.start()

    barrier = pltpu.get_barrier_semaphore()
    greet(barrier, me, 16, 8)
    greet(barrier, me, 4, 4)
    greet(barrier, me, 1, 4)

    half_width, centre, last_scale = chebyshev_scalars(bounds_ref)
    shift = 3.75 - centre
    factor = 2.0 / (24.0 * half_width)
    zero = jnp.zeros((rows, 8, GY), jnp.float32)

    def load_potential(group, _):
        for part in range(GROUP):
            z = group * GROUP + part
            for r in range(rows):
                diagonal[z, r] = 24.0 * (potential[z, pl.ds(r, 8, stride=rows), :] + shift)
        return 0

    for buffer in range(2):
        for z in (0, 1, planes + 2, planes + 3):
            buffers[buffer, z] = zero
    even, odd = buffers.at[0], buffers.at[1]
    matrix = circulant()
    for piece_number in range(pieces):
        loads[0][piece_number].wait()
        load_potential(piece_number, 0)
    toward = jnp.where(lax.axis_index("cuts") == 0, 1, -1)
    mine, level = lax.rem(me, PLANE_XY), lax.div(me, PLANE_XY)

    def at_level(number):
        return lax.rem(level + number + PLANES_Z, PLANES_Z) * PLANE_XY

    def to_float(state):
        def convert(group, _):
            for part in range(GROUP):
                z = group * GROUP + part
                start[state, z] = initial[state, z].astype(jnp.float32)
            return 0

        lax.fori_loop(0, planes // GROUP, convert, 0)

    lend = remote(start.at[1], start.at[2], lend_sem.at[0], lend_sem.at[1], at_level(toward) + mine)
    for load in loads[1]:
        load.wait()
    to_float(0)

    def one_turn(turn, _):
        @pl.when(turn == 2)
        def _():
            lend.wait()

        def load(group, _):
            for part in range(GROUP):
                z = group * GROUP + part
                for r in range(rows):
                    even[z + 2, r] = start[turn, z, pl.ds(r, 8, stride=rows), :]
                odd[z + 2] = zero
            return 0

        lax.fori_loop(0, planes // GROUP, load, 0)

        def two_steps(pair, _):
            first = jnp.where(pair == 0, 0.5 * factor, factor)
            filter_step(even, odd, diagonal, matrix, first)

            @pl.when((turn == 0) & (pair == 0))
            def _():
                pl.semaphore_wait(barrier, 7 + 3 + 3)
                greet(heard_x, me, 1, 4)
                for load in loads[2]:
                    load.wait()
                to_float(1)
                lend.start()

            @pl.when((turn == 0) & (pair == 3))
            def _():
                pl.semaphore_wait(heard_x, 3)
                greet(heard_y, me, 4, 4)

            filter_step(odd, even, diagonal, matrix, factor)
            return 0

        lax.fori_loop(0, DEGREE // 2 - 1, two_steps, 0)
        filter_step(even, odd, diagonal, matrix, factor)

        def finish(z, r, latest):
            outbox[pl.ds((turn * planes + z) * width + r, 8, stride=rows), :] = latest * last_scale

        filter_step(odd, even, diagonal, matrix, factor, finish)

        @pl.when(turn == 0)
        def _():
            pl.semaphore_wait(heard_y, 3)

        depth = jnp.where(turn == 0, PLANES_Z, PLANES_Z // 2)
        heading = jnp.where(turn == 1, -toward, toward)
        y, x = lax.div(mine, 4), lax.rem(mine, 4)

        def send_column(count, _):
            column = PLANE_XY - 1 - count
            beside = lax.rem(y + lax.div(column, 4), 4) * 4 + lax.rem(x + lax.rem(column, 4), 4)

            def send(count, _):
                number = depth - 1 - count
                peer = at_level(number * heading) + beside
                remote(
                    outbox.at[pl.ds((turn * devices + peer) * piece, piece)],
                    inbox.at[pl.ds(inbox_row(turn), piece)],
                    send_sem,
                    recv_sem.at[jnp.minimum(turn, 1)],
                    peer,
                ).start()
                return 0

            lax.fori_loop(0, jnp.where(column == 0, depth - 1, depth), send, 0)
            return 0

        lax.fori_loop(0, PLANE_XY, send_column, 0)
        own_copy(turn).start()
        return 0

    def inbox_row(turn):
        owner = jnp.where(turn == 2, at_level(-toward) + mine, me)
        return (owner * states + jnp.minimum(turn, 1)) * piece

    def own_copy(turn):
        return pltpu.make_async_copy(
            outbox.at[pl.ds((turn * devices + me) * piece, piece)],
            inbox.at[pl.ds(inbox_row(turn), piece)],
            own_sem.at[turn],
        )

    lax.fori_loop(0, states + 1, one_turn, 0)
    for turn in range(states + 1):
        own_copy(turn).wait()
    wait_bytes(inbox.at[pl.ds(0, (devices - 1) * piece)], recv_sem.at[0])
    wait_bytes(inbox.at[pl.ds(0, (devices - 2) * piece)], recv_sem.at[1])

    total = devices * states

    def gram_piece(column, _):
        here = inbox[pl.ds(column, total, stride=piece), :]
        block[:, pl.ds(pl.multiple_of(column * GY, GY), GY)] = here
        return 0

    lax.fori_loop(0, piece, gram_piece, 0)
    rows_copy = pltpu.make_async_copy(block, rows_ref, rows_sem)
    rows_copy.start()
    half = total // 2


    def part_of(ref, number):
        count = ref.shape[0] // PLANE_XY
        return pl.ds(pl.multiple_of(number * count, 8), count)

    def plane_peer(number):
        y, x = lax.div(mine, 4), lax.rem(mine, 4)
        return lax.rem(y + lax.div(number, 4), 4) * 4 + lax.rem(x + lax.rem(number, 4), 4)

    def first_round(which):
        source, target = partial[which], in_plane[which]

        def share(number, _):
            to = plane_peer(number)
            remote(
                source.at[part_of(source, to)],
                target.at[mine],
                sum_send.at[which, 0],
                sum_recv.at[which, 0],
                level * PLANE_XY + to,
            ).start()
            return 0

        lax.fori_loop(1, PLANE_XY, share, 0)
        target[mine] = source[part_of(source, mine), :]

    def total_of(ref):
        parts = [ref[number] for number in range(ref.shape[0])]
        while len(parts) > 1:
            parts = [parts[i] + parts[i + 1] for i in range(0, len(parts), 2)]
        return parts[0]

    def second_round(which):
        source, target = in_plane[which], in_column[which]
        wait_bytes(source.at[pl.ds(0, PLANE_XY - 1)], sum_recv.at[which, 0])
        target[level] = total_of(source)

        def along_z(number, _):
            remote(
                target.at[level],
                target.at[level],
                sum_send.at[which, 1],
                sum_recv.at[which, 1],
                lax.rem(level + number, PLANES_Z) * PLANE_XY + mine,
            ).start()
            return 0

        lax.fori_loop(1, PLANES_Z, along_z, 0)

    def third_round(which):
        source, target = in_column[which], gathered[which]
        wait_bytes(source.at[pl.ds(0, PLANES_Z - 1)], sum_recv.at[which, 1])
        here = part_of(target, mine)
        target[here, :] = total_of(source)

        def spread(number, _):
            remote(
                target.at[here],
                target.at[here],
                sum_send.at[which, 2],
                sum_recv.at[which, 2],
                level * PLANE_XY + plane_peer(number),
            ).start()
            return 0

        lax.fori_loop(1, PLANE_XY, spread, 0)

    def most_of(ref):
        return ref.at[pl.ds(0, ref.shape[0] // PLANE_XY * (PLANE_XY - 1))]

    partial[0][...] = times(block[0:half], block[0:half], 1, 1)
    first_round(0)
    partial[1][0:half] = times(block[half:], block[0:half], 1, 1)
    partial[1][half:] = times(block[half:], block[half:], 1, 1)
    first_round(1)
    second_round(0)
    second_round(1)
    third_round(0)
    third_round(1)
    wait_bytes(most_of(gathered[0]), sum_recv.at[0, 2])
    tiles = inverse_factor([gathered[0][8 * i : 8 * i + 8] for i in range(16)])
    for i in range(16):
        first_ref[8 * i : 8 * i + 8] = tiles[i]
    wait_bytes(most_of(gathered[1]), sum_recv.at[1, 2])
    low = times(gathered[1][0:half], first_ref[...], 1, 1)
    low_ref[...] = low
    rest_ref[...] = gathered[1][half:] - times(low, low, 1, 1)
    for which in range(2):
        wait_bytes(in_plane[which].at[pl.ds(0, PLANE_XY - 1)], sum_send.at[which, 0])
        wait_bytes(in_column[which].at[pl.ds(0, PLANES_Z - 1)], sum_send.at[which, 1])
        wait_bytes(most_of(gathered[which]), sum_send.at[which, 2])
    rows_copy.wait()
    wait_bytes(outbox.at[pl.ds(0, (2 * devices - 3) * piece)], send_sem)


def filter_and_gram(states, potential, bounds):
    count, planes, width = states.shape[:3]
    total, half = count * 128, count * 64
    points = planes * width * GY // 128
    return pl.pallas_call(
        filter_gram_kernel,
        out_shape=[
            jax.ShapeDtypeStruct((total, points), jnp.float32),
            jax.ShapeDtypeStruct((half, half), jnp.float32),
            jax.ShapeDtypeStruct((half, half), jnp.float32),
            jax.ShapeDtypeStruct((half, half), jnp.float32),
        ],
        in_specs=[
            pl.BlockSpec(memory_space=pltpu.SMEM),
            pl.BlockSpec(memory_space=pl.ANY),
            pl.BlockSpec(memory_space=pl.ANY),
        ],
        out_specs=[pl.BlockSpec(memory_space=pl.ANY)] + [pl.BlockSpec(memory_space=pltpu.VMEM)] * 3,
        scratch_shapes=[
            pltpu.VMEM(states.shape, states.dtype),
            pltpu.VMEM(potential.shape, potential.dtype),
            pltpu.VMEM((2, planes + 4, width // 8, 8, GY), jnp.float32),
            pltpu.VMEM((planes, width // 8, 8, GY), jnp.float32),
            pltpu.VMEM((count + 1, planes, width, GY), jnp.float32),
            pltpu.VMEM(((count + 1) * planes * width, GY), jnp.float32),
            pltpu.VMEM((count * planes * width, GY), jnp.float32),
            pltpu.VMEM((total, points), jnp.float32),
            pltpu.VMEM((half, GY), jnp.float32),
            pltpu.VMEM((total, GY), jnp.float32),
            pltpu.VMEM((PLANE_XY, half // PLANE_XY, GY), jnp.float32),
            pltpu.VMEM((PLANE_XY, total // PLANE_XY, GY), jnp.float32),
            pltpu.VMEM((PLANES_Z, half // PLANE_XY, GY), jnp.float32),
            pltpu.VMEM((PLANES_Z, total // PLANE_XY, GY), jnp.float32),
            pltpu.VMEM((half, GY), jnp.float32),
            pltpu.VMEM((total, GY), jnp.float32),
            pltpu.SemaphoreType.DMA,
            pltpu.SemaphoreType.DMA((2,)),
            pltpu.SemaphoreType.DMA((count + 1,)),
            pltpu.SemaphoreType.DMA,
            pltpu.SemaphoreType.DMA((2, 3)),
            pltpu.SemaphoreType.DMA((2, 3)),
            pltpu.SemaphoreType.DMA((count + 1, planes // GROUP)),
            pltpu.SemaphoreType.DMA((2,)),
            pltpu.SemaphoreType.REGULAR,
            pltpu.SemaphoreType.REGULAR,
        ],
        compiler_params=pltpu.CompilerParams(
            vmem_limit_bytes=56 << 20, collective_id=0, has_side_effects=True
        ),
        name="filter_and_gram",
    )(bounds, states, potential)


def times(left, right, left_dim, right_dim):
    return lax.dot_general(
        left,
        right,
        (((left_dim,), (right_dim,)), ((), ())),
        precision=lax.Precision.HIGHEST,
        preferred_element_type=jnp.float32,
    )


def inverse_factor(tiles, beside=None):
    row = lax.broadcasted_iota(jnp.int32, (8, 128), 0)
    lane = lax.broadcasted_iota(jnp.int32, (8, 128), 1)

    def of_row(value, index):
        return jnp.broadcast_to(value[index : index + 1, :], (8, 128))

    def of_lane(value, index):
        return jnp.broadcast_to(value[:, index : index + 1], (8, 128))

    tiles = list(tiles)
    result = []
    for tile in range(16):
        start = 8 * tile
        here = tiles[tile]
        solved = jnp.zeros((8, 128), jnp.float32)
        columns = [of_lane(here, start + c) for c in range(8)]
        below = range(tile + 1, 16)
        multipliers = [[of_lane(tiles[i], start + c) for c in range(8)] for i in below]
        inverses = []
        for i in range(8):
            pivot = of_row(columns[i], i)
            inverses.append(1.0 / pivot)
            here = jnp.where(lane == start + i, jnp.where(row == i, 1.0, 0.0), here)
            pivot_row = of_row(here, i)
            solved = jnp.where(row == i, pivot_row * lax.rsqrt(pivot), solved)
            others = jnp.where(row == i, 0.0, columns[i])
            here = here - (others * pivot_row) * inverses[i]
            for c in range(i + 1, 8):
                columns[c] = columns[c] - (others * of_row(columns[c], i)) * inverses[i]
        result.append(jnp.where(lane <= start + row, solved, 0.0))
        spread = [of_row(here, c) * inverses[c] for c in range(8)]
        for multiplier, i in zip(multipliers, below):
            parts = [multiplier[c] * spread[c] for c in range(8)]
            total = ((parts[0] + parts[1]) + (parts[2] + parts[3])) + (
                (parts[4] + parts[5]) + (parts[6] + parts[7])
            )
            tiles[i] = jnp.where((lane >= start) & (lane < start + 8), 0.0, tiles[i]) - total
        if beside is not None:
            beside(tile)
    return result


def solve_kernel(
    first_ref, low_ref, rest_ref, rows_ref, out_ref, second, rows, out, rows_sem, out_sem, *, scale
):
    half = first_ref.shape[0]
    width = rows_ref.shape[1]
    loads = []
    for number in range(rows_sem.shape[0]):
        here = pl.ds(number * width // rows_sem.shape[0], width // rows_sem.shape[0])
        loads.append(pltpu.make_async_copy(rows_ref.at[:, here], rows.at[:, here], rows_sem.at[number]))
        loads[number].start()
    first_piece = 16 - width // 128
    per_load = width // 128 // len(loads)

    def beside(tile):
        if tile < first_piece:
            return
        if (tile - first_piece) % per_load == 0:
            loads[(tile - first_piece) // per_load].wait()
        here = pl.ds((tile - first_piece) * 128, 128)
        upper = times(first_ref[...], rows[0:half, here], 1, 0)
        out[0:half, here] = upper * scale
        rows[half:, here] = rows[half:, here] - times(low_ref[...], upper, 1, 0)

    tiles = inverse_factor([rest_ref[8 * i : 8 * i + 8] for i in range(16)], beside)
    upper_store = pltpu.make_async_copy(
        out.at[0:half], out_ref.at[0:half], out_sem.at[out_sem.shape[0] - 1]
    )
    upper_store.start()
    for i in range(16):
        second[8 * i : 8 * i + 8] = tiles[i] * scale
    pieces = out_sem.shape[0] - 1
    stores = [upper_store]
    for piece in range(pieces):
        here = pl.ds(piece * width // pieces, width // pieces)
        out[half:, here] = times(second[...], rows[half:, here], 1, 0)
        store = pltpu.make_async_copy(
            out.at[half:, here], out_ref.at[half:, here], out_sem.at[piece]
        )
        store.start()
        stores.append(store)
    for store in stores:
        store.wait()


def solve(first, low, rest, rows, scale):
    half = first.shape[0]
    return pl.pallas_call(
        functools.partial(solve_kernel, scale=scale),
        out_shape=jax.ShapeDtypeStruct(rows.shape, jnp.float32),
        in_specs=[pl.BlockSpec(memory_space=pltpu.VMEM)] * 3 + [pl.BlockSpec(memory_space=pl.ANY)],
        out_specs=pl.BlockSpec(memory_space=pl.ANY),
        scratch_shapes=[
            pltpu.VMEM((half, half), jnp.float32),
            pltpu.VMEM(rows.shape, jnp.float32),
            pltpu.VMEM(rows.shape, jnp.float32),
            pltpu.SemaphoreType.DMA((4,)),
            pltpu.SemaphoreType.DMA((4,)),
        ],
        compiler_params=pltpu.CompilerParams(vmem_limit_bytes=56 << 20),
        name="solve",
    )(first, low, rest, rows)


def per_device(initial_states, potential, bounds):
    row_block, first, low, rest = filter_and_gram(initial_states, potential, bounds)
    return solve(first, low, rest, row_block, math.sqrt(math.prod(initial_states.shape[1:])))


def solution(mesh):
    return jax.shard_map(
        per_device,
        mesh=mesh,
        in_specs=(P(("cuts", "state"), None, None, None), P(), P("cuts")),
        out_specs=P("cuts", "state"),
        check_vma=False,
    )
```

```python
import functools
import math

import jax
import jax.numpy as jnp
from jax import lax
from jax.experimental import pallas as pl
from jax.experimental.pallas import tpu as pltpu
from jax.sharding import PartitionSpec as P

DEGREE = 16
ANCHOR_VALUE = -1.125
XB = 8
GY = 128


def chebyshev_scalars(bounds_ref):
    low_end = jnp.full((8, GY), bounds_ref[0].astype(jnp.float32), jnp.float32) / 64.0
    high_end = jnp.full((8, GY), bounds_ref[1].astype(jnp.float32), jnp.float32) / 16.0
    half_width = (high_end - low_end) / 2.0
    centre = (high_end + low_end) / 2.0
    place = (ANCHOR_VALUE - centre) / half_width
    before, now = jnp.ones_like(place), place
    for _ in range(DEGREE - 1):
        before, now = now, 2.0 * place * now - before
    return half_width, centre, 1.0 / now


def circulant():
    row = lax.broadcasted_iota(jnp.int32, (2 * GY, GY), 0)
    column = lax.broadcasted_iota(jnp.int32, (2 * GY, GY), 1)
    apart = jnp.bitwise_and(row - column, GY - 1)
    near = jnp.where((apart == 1) | (apart == GY - 1), -16.0, 0.0)
    far = jnp.where((apart == 2) | (apart == GY - 2), 1.0, 0.0)
    return (near + far).astype(jnp.bfloat16)


def filter_step(source, target, diagonal, matrix, factor, finish=None):
    planes, rows = diagonal.shape[0], diagonal.shape[1]
    values = source[pl.ds(2, planes)].reshape(planes * rows * 8, GY)
    high = values.astype(jnp.bfloat16)
    low = (values - high.astype(jnp.float32)).astype(jnp.bfloat16)
    along_y = jnp.dot(
        jnp.concatenate([high, low], 1), matrix, preferred_element_type=jnp.float32
    ).reshape(planes, rows, 8, GY)
    for z in range(planes):
        here = [source[z + 2, r] for r in range(rows)]
        ring = (
            [pltpu.roll(here[r], 1, 0) for r in (rows - 2, rows - 1)]
            + here
            + [pltpu.roll(here[r], 7, 0) for r in (0, 1)]
        )
        for r in range(rows):
            near = (source[z + 1, r] + source[z + 3, r]) + (ring[r + 1] + ring[r + 3])
            far = (source[z, r] + source[z + 4, r]) + (ring[r] + ring[r + 4])
            total = far - 16.0 * near + diagonal[z, r] * here[r] + along_y[z, r]
            latest = factor * total - target[z + 2, r]
            if finish is None:
                target[z + 2, r] = latest
            else:
                finish(z, r, latest)


GROUP = 8
PLANES_Z = 8
PLANE_XY = 16


def along(me, stride, extent, number):
    place = lax.rem(lax.div(me, stride), extent)
    return me + (lax.rem(place + number, extent) - place) * stride


def greet(semaphore, me, stride, extent):
    for number in range(1, extent):
        pl.semaphore_signal(
            semaphore,
            inc=1,
            device_id={"state": along(me, stride, extent, number)},
            device_id_type=pl.DeviceIdType.MESH,
        )


def remote(source, target, send, receive, peer):
    return pltpu.make_async_remote_copy(
        src_ref=source,
        dst_ref=target,
        send_sem=send,
        recv_sem=receive,
        device_id={"state": peer},
        device_id_type=pl.DeviceIdType.MESH,
    )


def wait_bytes(ref, semaphore):
    pltpu.make_async_copy(ref, ref, semaphore).wait()


def filter_gram_kernel(
    bounds_ref,
    states_ref,
    potential_ref,
    rows_ref,
    first_ref,
    low_ref,
    rest_ref,
    initial,
    potential,
    buffers,
    diagonal,
    start,
    outbox,
    inbox,
    block,
    partial_first,
    partial_rest,
    plane_first,
    plane_rest,
    column_first,
    column_rest,
    gathered_first,
    gathered_rest,
    send_sem,
    recv_sem,
    own_sem,
    rows_sem,
    sum_send,
    sum_recv,
    load_sem,
    lend_sem,
    heard_x,
    heard_y,
):
    partial, in_plane = (partial_first, partial_rest), (plane_first, plane_rest)
    in_column, gathered = (column_first, column_rest), (gathered_first, gathered_rest)
    states, planes, width, _ = states_ref.shape
    rows = width // 8
    devices = 128
    piece = planes * width // devices
    me = lax.axis_index("state")

    pieces = planes // GROUP
    loads = []
    for number, (source, target) in enumerate(
        [(potential_ref, potential)]
        + [(states_ref.at[state], initial.at[state]) for state in range(states)]
    ):
        here = [pl.ds(piece * GROUP, GROUP) for piece in range(pieces)]
        loads.append(
            [
                pltpu.make_async_copy(source.at[here[i]], target.at[here[i]], load_sem.at[number, i])
                for i in range(pieces)
            ]
        )

    for number in (2, 0, 1):
        for load in loads[number]:
            load.start()

    barrier = pltpu.get_barrier_semaphore()
    greet(barrier, me, 16, 8)
    greet(barrier, me, 4, 4)
    greet(barrier, me, 1, 4)

    half_width, centre, last_scale = chebyshev_scalars(bounds_ref)
    shift = 3.75 - centre
    factor = 2.0 / (24.0 * half_width)
    zero = jnp.zeros((rows, 8, GY), jnp.float32)

    def load_potential(group, _):
        for part in range(GROUP):
            z = group * GROUP + part
            for r in range(rows):
                diagonal[z, r] = 24.0 * (potential[z, pl.ds(r, 8, stride=rows), :] + shift)
        return 0

    for buffer in range(2):
        for z in (0, 1, planes + 2, planes + 3):
            buffers[buffer, z] = zero
    even, odd = buffers.at[0], buffers.at[1]
    matrix = circulant()
    toward = jnp.where(lax.axis_index("cuts") == 0, 1, -1)
    mine, level = lax.rem(me, PLANE_XY), lax.div(me, PLANE_XY)

    def at_level(number):
        return lax.rem(level + number + PLANES_Z, PLANES_Z) * PLANE_XY

    def to_float(state):
        def convert(group, _):
            for part in range(GROUP):
                z = group * GROUP + part
                start[state, z] = initial[state, z].astype(jnp.float32)
            return 0

        lax.fori_loop(0, planes // GROUP, convert, 0)

    lend = remote(start.at[1], start.at[2], lend_sem.at[0], lend_sem.at[1], at_level(toward) + mine)
    for load in loads[2]:
        load.wait()
    to_float(1)
    pl.semaphore_wait(barrier, 7 + 3 + 3)
    lend.start()
    greet(heard_x, me, 1, 4)

    for piece_number in range(pieces):
        loads[0][piece_number].wait()
        load_potential(piece_number, 0)
    for load in loads[1]:
        load.wait()
    to_float(0)

    def one_turn(turn, _):
        @pl.when(turn == 2)
        def _():
            lend.wait()

        def load(group, _):
            for part in range(GROUP):
                z = group * GROUP + part
                for r in range(rows):
                    even[z + 2, r] = start[turn, z, pl.ds(r, 8, stride=rows), :]
                odd[z + 2] = zero
            return 0

        lax.fori_loop(0, planes // GROUP, load, 0)

        def two_steps(pair, _):
            first = jnp.where(pair == 0, 0.5 * factor, factor)
            filter_step(even, odd, diagonal, matrix, first)

            @pl.when((turn == 0) & (pair == 3))
            def _():
                pl.semaphore_wait(heard_x, 3)
                greet(heard_y, me, 4, 4)

            filter_step(odd, even, diagonal, matrix, factor)
            return 0

        lax.fori_loop(0, DEGREE // 2 - 1, two_steps, 0)
        filter_step(even, odd, diagonal, matrix, factor)

        def finish(z, r, latest):
            outbox[pl.ds((turn * planes + z) * width + r, 8, stride=rows), :] = latest * last_scale

        filter_step(odd, even, diagonal, matrix, factor, finish)

        @pl.when(turn == 0)
        def _():
            pl.semaphore_wait(heard_y, 3)

        depth = jnp.where(turn == 0, PLANES_Z, PLANES_Z // 2)
        heading = jnp.where(turn == 1, -toward, toward)
        y, x = lax.div(mine, 4), lax.rem(mine, 4)

        def send_column(count, _):
            column = PLANE_XY - 1 - count
            beside = lax.rem(y + lax.div(column, 4), 4) * 4 + lax.rem(x + lax.rem(column, 4), 4)

            def send(count, _):
                number = depth - 1 - count
                peer = at_level(number * heading) + beside
                remote(
                    outbox.at[pl.ds((turn * devices + peer) * piece, piece)],
                    inbox.at[pl.ds(inbox_row(turn), piece)],
                    send_sem,
                    recv_sem.at[jnp.minimum(turn, 1)],
                    peer,
                ).start()
                return 0

            lax.fori_loop(0, jnp.where(column == 0, depth - 1, depth), send, 0)
            return 0

        lax.fori_loop(0, PLANE_XY, send_column, 0)
        own_copy(turn).start()
        return 0

    def inbox_row(turn):
        owner = jnp.where(turn == 2, at_level(-toward) + mine, me)
        return (owner * states + jnp.minimum(turn, 1)) * piece

    def own_copy(turn):
        return pltpu.make_async_copy(
            outbox.at[pl.ds((turn * devices + me) * piece, piece)],
            inbox.at[pl.ds(inbox_row(turn), piece)],
            own_sem.at[turn],
        )

    lax.fori_loop(0, states + 1, one_turn, 0)
    for turn in range(states + 1):
        own_copy(turn).wait()
    wait_bytes(inbox.at[pl.ds(0, (devices - 1) * piece)], recv_sem.at[0])
    wait_bytes(inbox.at[pl.ds(0, (devices - 2) * piece)], recv_sem.at[1])

    total = devices * states

    def gram_piece(column, _):
        here = inbox[pl.ds(column, total, stride=piece), :]
        block[:, pl.ds(pl.multiple_of(column * GY, GY), GY)] = here
        return 0

    lax.fori_loop(0, piece, gram_piece, 0)
    rows_copy = pltpu.make_async_copy(block, rows_ref, rows_sem)
    rows_copy.start()
    half = total // 2


    def part_of(ref, number):
        count = ref.shape[0] // PLANE_XY
        return pl.ds(pl.multiple_of(number * count, 8), count)

    def plane_peer(number):
        y, x = lax.div(mine, 4), lax.rem(mine, 4)
        return lax.rem(y + lax.div(number, 4), 4) * 4 + lax.rem(x + lax.rem(number, 4), 4)

    def first_round(which):
        source, target = partial[which], in_plane[which]

        def share(number, _):
            to = plane_peer(number)
            remote(
                source.at[part_of(source, to)],
                target.at[mine],
                sum_send.at[which, 0],
                sum_recv.at[which, 0],
                level * PLANE_XY + to,
            ).start()
            return 0

        lax.fori_loop(1, PLANE_XY, share, 0)
        target[mine] = source[part_of(source, mine), :]

    def total_of(ref):
        parts = [ref[number] for number in range(ref.shape[0])]
        while len(parts) > 1:
            parts = [parts[i] + parts[i + 1] for i in range(0, len(parts), 2)]
        return parts[0]

    def second_round(which):
        source, target = in_plane[which], in_column[which]
        wait_bytes(source.at[pl.ds(0, PLANE_XY - 1)], sum_recv.at[which, 0])
        target[level] = total_of(source)

        def along_z(number, _):
            remote(
                target.at[level],
                target.at[level],
                sum_send.at[which, 1],
                sum_recv.at[which, 1],
                lax.rem(level + number, PLANES_Z) * PLANE_XY + mine,
            ).start()
            return 0

        lax.fori_loop(1, PLANES_Z, along_z, 0)

    def third_round(which):
        source, target = in_column[which], gathered[which]
        wait_bytes(source.at[pl.ds(0, PLANES_Z - 1)], sum_recv.at[which, 1])
        here = part_of(target, mine)
        target[here, :] = total_of(source)

        def spread(number, _):
            remote(
                target.at[here],
                target.at[here],
                sum_send.at[which, 2],
                sum_recv.at[which, 2],
                level * PLANE_XY + plane_peer(number),
            ).start()
            return 0

        lax.fori_loop(1, PLANE_XY, spread, 0)

    def most_of(ref):
        return ref.at[pl.ds(0, ref.shape[0] // PLANE_XY * (PLANE_XY - 1))]

    partial[0][...] = times(block[0:half], block[0:half], 1, 1)
    first_round(0)
    partial[1][0:half] = times(block[half:], block[0:half], 1, 1)
    partial[1][half:] = times(block[half:], block[half:], 1, 1)
    first_round(1)
    second_round(0)
    second_round(1)
    third_round(0)
    third_round(1)
    wait_bytes(most_of(gathered[0]), sum_recv.at[0, 2])
    tiles = inverse_factor([gathered[0][8 * i : 8 * i + 8] for i in range(16)])
    for i in range(16):
        first_ref[8 * i : 8 * i + 8] = tiles[i]
    wait_bytes(most_of(gathered[1]), sum_recv.at[1, 2])
    low = times(gathered[1][0:half], first_ref[...], 1, 1)
    low_ref[...] = low
    rest_ref[...] = gathered[1][half:] - times(low, low, 1, 1)
    for which in range(2):
        wait_bytes(in_plane[which].at[pl.ds(0, PLANE_XY - 1)], sum_send.at[which, 0])
        wait_bytes(in_column[which].at[pl.ds(0, PLANES_Z - 1)], sum_send.at[which, 1])
        wait_bytes(most_of(gathered[which]), sum_send.at[which, 2])
    rows_copy.wait()
    wait_bytes(outbox.at[pl.ds(0, (2 * devices - 3) * piece)], send_sem)


def filter_and_gram(states, potential, bounds):
    count, planes, width = states.shape[:3]
    total, half = count * 128, count * 64
    points = planes * width * GY // 128
    return pl.pallas_call(
        filter_gram_kernel,
        out_shape=[
            jax.ShapeDtypeStruct((total, points), jnp.float32),
            jax.ShapeDtypeStruct((half, half), jnp.float32),
            jax.ShapeDtypeStruct((half, half), jnp.float32),
            jax.ShapeDtypeStruct((half, half), jnp.float32),
        ],
        in_specs=[
            pl.BlockSpec(memory_space=pltpu.SMEM),
            pl.BlockSpec(memory_space=pl.ANY),
            pl.BlockSpec(memory_space=pl.ANY),
        ],
        out_specs=[pl.BlockSpec(memory_space=pl.ANY)] + [pl.BlockSpec(memory_space=pltpu.VMEM)] * 3,
        scratch_shapes=[
            pltpu.VMEM(states.shape, states.dtype),
            pltpu.VMEM(potential.shape, potential.dtype),
            pltpu.VMEM((2, planes + 4, width // 8, 8, GY), jnp.float32),
            pltpu.VMEM((planes, width // 8, 8, GY), jnp.float32),
            pltpu.VMEM((count + 1, planes, width, GY), jnp.float32),
            pltpu.VMEM(((count + 1) * planes * width, GY), jnp.float32),
            pltpu.VMEM((count * planes * width, GY), jnp.float32),
            pltpu.VMEM((total, points), jnp.float32),
            pltpu.VMEM((half, GY), jnp.float32),
            pltpu.VMEM((total, GY), jnp.float32),
            pltpu.VMEM((PLANE_XY, half // PLANE_XY, GY), jnp.float32),
            pltpu.VMEM((PLANE_XY, total // PLANE_XY, GY), jnp.float32),
            pltpu.VMEM((PLANES_Z, half // PLANE_XY, GY), jnp.float32),
            pltpu.VMEM((PLANES_Z, total // PLANE_XY, GY), jnp.float32),
            pltpu.VMEM((half, GY), jnp.float32),
            pltpu.VMEM((total, GY), jnp.float32),
            pltpu.SemaphoreType.DMA,
            pltpu.SemaphoreType.DMA((2,)),
            pltpu.SemaphoreType.DMA((count + 1,)),
            pltpu.SemaphoreType.DMA,
            pltpu.SemaphoreType.DMA((2, 3)),
            pltpu.SemaphoreType.DMA((2, 3)),
            pltpu.SemaphoreType.DMA((count + 1, planes // GROUP)),
            pltpu.SemaphoreType.DMA((2,)),
            pltpu.SemaphoreType.REGULAR,
            pltpu.SemaphoreType.REGULAR,
        ],
        compiler_params=pltpu.CompilerParams(
            vmem_limit_bytes=56 << 20, collective_id=0, has_side_effects=True
        ),
        name="filter_and_gram",
    )(bounds, states, potential)


def times(left, right, left_dim, right_dim):
    return lax.dot_general(
        left,
        right,
        (((left_dim,), (right_dim,)), ((), ())),
        precision=lax.Precision.HIGHEST,
        preferred_element_type=jnp.float32,
    )


def inverse_factor(tiles, beside=None):
    row = lax.broadcasted_iota(jnp.int32, (8, 128), 0)
    lane = lax.broadcasted_iota(jnp.int32, (8, 128), 1)

    def of_row(value, index):
        return jnp.broadcast_to(value[index : index + 1, :], (8, 128))

    def of_lane(value, index):
        return jnp.broadcast_to(value[:, index : index + 1], (8, 128))

    tiles = list(tiles)
    result = []
    for tile in range(16):
        start = 8 * tile
        here = tiles[tile]
        solved = jnp.zeros((8, 128), jnp.float32)
        columns = [of_lane(here, start + c) for c in range(8)]
        below = range(tile + 1, 16)
        multipliers = [[of_lane(tiles[i], start + c) for c in range(8)] for i in below]
        inverses = []
        for i in range(8):
            pivot = of_row(columns[i], i)
            inverses.append(1.0 / pivot)
            here = jnp.where(lane == start + i, jnp.where(row == i, 1.0, 0.0), here)
            pivot_row = of_row(here, i)
            solved = jnp.where(row == i, pivot_row * lax.rsqrt(pivot), solved)
            others = jnp.where(row == i, 0.0, columns[i])
            here = here - (others * pivot_row) * inverses[i]
            for c in range(i + 1, 8):
                columns[c] = columns[c] - (others * of_row(columns[c], i)) * inverses[i]
        result.append(jnp.where(lane <= start + row, solved, 0.0))
        spread = [of_row(here, c) * inverses[c] for c in range(8)]
        for multiplier, i in zip(multipliers, below):
            parts = [multiplier[c] * spread[c] for c in range(8)]
            total = ((parts[0] + parts[1]) + (parts[2] + parts[3])) + (
                (parts[4] + parts[5]) + (parts[6] + parts[7])
            )
            tiles[i] = jnp.where((lane >= start) & (lane < start + 8), 0.0, tiles[i]) - total
        if beside is not None:
            beside(tile)
    return result


def solve_kernel(
    first_ref, low_ref, rest_ref, rows_ref, out_ref, second, rows, out, rows_sem, out_sem, *, scale
):
    half = first_ref.shape[0]
    width = rows_ref.shape[1]
    loads = []
    for number in range(rows_sem.shape[0]):
        here = pl.ds(number * width // rows_sem.shape[0], width // rows_sem.shape[0])
        loads.append(pltpu.make_async_copy(rows_ref.at[:, here], rows.at[:, here], rows_sem.at[number]))
        loads[number].start()
    first_piece = 16 - width // 128
    per_load = width // 128 // len(loads)

    def beside(tile):
        if tile < first_piece:
            return
        if (tile - first_piece) % per_load == 0:
            loads[(tile - first_piece) // per_load].wait()
        here = pl.ds((tile - first_piece) * 128, 128)
        upper = times(first_ref[...], rows[0:half, here], 1, 0)
        out[0:half, here] = upper * scale
        rows[half:, here] = rows[half:, here] - times(low_ref[...], upper, 1, 0)

    tiles = inverse_factor([rest_ref[8 * i : 8 * i + 8] for i in range(16)], beside)
    upper_store = pltpu.make_async_copy(
        out.at[0:half], out_ref.at[0:half], out_sem.at[out_sem.shape[0] - 1]
    )
    upper_store.start()
    for i in range(16):
        second[8 * i : 8 * i + 8] = tiles[i] * scale
    pieces = out_sem.shape[0] - 1
    stores = [upper_store]
    for piece in range(pieces):
        here = pl.ds(piece * width // pieces, width // pieces)
        out[half:, here] = times(second[...], rows[half:, here], 1, 0)
        store = pltpu.make_async_copy(
            out.at[half:, here], out_ref.at[half:, here], out_sem.at[piece]
        )
        store.start()
        stores.append(store)
    for store in stores:
        store.wait()


def solve(first, low, rest, rows, scale):
    half = first.shape[0]
    return pl.pallas_call(
        functools.partial(solve_kernel, scale=scale),
        out_shape=jax.ShapeDtypeStruct(rows.shape, jnp.float32),
        in_specs=[pl.BlockSpec(memory_space=pltpu.VMEM)] * 3 + [pl.BlockSpec(memory_space=pl.ANY)],
        out_specs=pl.BlockSpec(memory_space=pl.ANY),
        scratch_shapes=[
            pltpu.VMEM((half, half), jnp.float32),
            pltpu.VMEM(rows.shape, jnp.float32),
            pltpu.VMEM(rows.shape, jnp.float32),
            pltpu.SemaphoreType.DMA((4,)),
            pltpu.SemaphoreType.DMA((4,)),
        ],
        compiler_params=pltpu.CompilerParams(vmem_limit_bytes=56 << 20),
        name="solve",
    )(first, low, rest, rows)


def per_device(initial_states, potential, bounds):
    row_block, first, low, rest = filter_and_gram(initial_states, potential, bounds)
    return solve(first, low, rest, row_block, math.sqrt(math.prod(initial_states.shape[1:])))


def solution(mesh):
    return jax.shard_map(
        per_device,
        mesh=mesh,
        in_specs=(P(("cuts", "state"), None, None, None), P(), P("cuts")),
        out_specs=P("cuts", "state"),
        check_vma=False,
    )
```
